32 devices in a mesh: blk: 8 (over z, y), trk: 4 (over x, core).
Axes of the slice: x: 2, y: 2, z: 4, core: 2. Of those that a mesh axis runs over, the one named last changes fastest.
Arguments:
- row_block: int32 [8192, 1], P(('blk', 'trk')), may hold values from 0 to 7; in each aligned block of 256 rows (0 to 255, 256 to 511, ...) at most 64 rows name the same one
- row_hits: int32 [2, 8192], P(None, ('blk', 'trk')), may hold values from 0 to 63
- row_slot: int32 [8192], P(('blk', 'trk')), may hold values from 0 to 4
- track_kept: int32 [1024], P(('blk', 'trk')), may hold values 0 or 1
- row_derivs: bfloat16 [12, 8192], P(None, ('blk', 'trk')), may hold values from -0.75 to 0.75
- row_resid: bfloat16 [8192], P(('blk', 'trk')), may hold values from -6 to 6
- row_invsig: bfloat16 [8192], P(('blk', 'trk')), may hold values from 0.5 to 2
- pattern: int32 [8, 5], P('blk'), may hold values from 0 to 7, as said below
- prior: float32 [8, 384], P('blk'), may hold values from 0.2 to 3
Outputs:
- solution: float32 [8, 384], P('blk')
- gradient: float32 [8, 384], P('blk')
The draws below stay inside these ranges and needn't reach their ends.
Inputs may be any that keep to these rules, and one draw needn't show every extreme that they name: `row_block`: among the rows of one device (aligned blocks of 256 rows) no block is named by more than 64 rows, and in every draw some device's rows name some block exactly 64 times. `pattern`: row k lists the blocks k - 2, k - 1, k, k + 1, k + 2 modulo 8, each once, in an order of its own.
All inputs are finite; a program needn't handle non-finite values. No bound on the sum of `track_kept` on one device may be relied on, other than what follows from the above.
Results may differ from the reference program's by a relative error of at most 0.0036.
The reference program's roundings to bfloat16 on the way (of `scaled` and `weighted`) count: a program that leaves them out, or rounds other values in their place, can miss the bound.
Values may be sent and summed in bfloat16 or wider, within the bound.
A program may use at most 64 MiB of HBM per device.

```python
import math
import jax
import jax.numpy as jnp
import numpy as np
from jax import lax

MODS = 64
PAR = 6
NB = 5
SEG = 8
ITERS = 2
ROW_DEV = 256
ORDER = 384
NBLK = 8
CAP = 64
ROWS = 8192
TRACKS = 1024


def draw_pattern(key, part):
    keys = jax.random.split(key, NBLK)
    orders = jax.vmap(lambda one_key: jax.random.permutation(one_key, NB))(keys)
    offsets = orders.astype(jnp.int32) - NB // 2
    return (jnp.arange(NBLK, dtype=jnp.int32)[:, None] + offsets) % NBLK


def draw_prior(key, part):
    position = jnp.arange(NBLK, dtype=jnp.float32)[:, None] / max(NBLK - 1, 1)
    rising = 1.0 + 2.0 * position
    base = jnp.exp(jax.random.uniform(key, (NBLK, ORDER), jnp.float32, math.log(0.2), 0.0))
    return base * rising


def with_ends(result, key, low, top_value):
    dims = result.shape
    place = [jax.random.randint(jax.random.fold_in(key, axis), (), 0, dims[axis]) for axis in range(len(dims))]
    result = result.at[tuple(place)].set(low)
    longest = dims.index(max(dims))
    place[longest] = (place[longest] + 1) % dims[longest]
    return result.at[tuple(place)].set(top_value)


def block_scale(key, extent, cuts, least, high):
    factor_of, own = 1.0, jax.random.fold_in(key, 6)
    for dim, parts in cuts:
        draws = jnp.exp(jax.random.uniform(jax.random.fold_in(own, dim), (parts,), jnp.float32, least / len(cuts), high / len(cuts)))
        factor_of = factor_of * jnp.repeat(draws, extent[dim] // parts).reshape([-1 if axis == dim else 1 for axis in range(len(extent))])
    return factor_of


def routed_block(own_key, own, number, rows, number_of, top, reach, skew):
    sequence = jax.random.permutation(own_key, number_of)
    crowded, usual = shares(number_of, rows * top, reach, skew, True), shares(number_of, rows * top, reach, skew, False)
    places = jnp.arange(number_of)

    def named(lengths, offset_by):
        used = int((lengths > 0).sum())
        fixed = max(1, used // 4)
        shifted = fixed + (places - fixed + offset_by * (used - fixed)) % max(1, number_of - fixed)
        return jnp.zeros((number_of,), jnp.int32).at[sequence[jnp.where(places < fixed, places, shifted)]].set(jnp.asarray(lengths, jnp.int32))

    lengths = jnp.where(number % 4 == 0, named(crowded, number // 4), named(usual, number - number // 4 - 1))
    mixed = jax.random.permutation(jax.random.fold_in(own, 3), number_of)
    donor, taker = mixed[0:number_of // 2 * 2:2], mixed[1:number_of // 2 * 2:2]
    margin = jnp.minimum(lengths[donor] - 1, reach - lengths[taker]) // 2
    margin = jnp.where((donor == sequence[0]) | (taker == sequence[0]) | (lengths[taker] == 0), 0, jnp.maximum(margin, 0))
    shifted = jax.random.randint(jax.random.fold_in(own, 4), (number_of // 2,), 0, 1 << 20) % (margin + 1)
    lengths = lengths.at[donor].add(-shifted).at[taker].add(shifted)
    items = jnp.searchsorted(jnp.cumsum(lengths), jnp.arange(rows * top), side="right").astype(jnp.int32)
    table = items.reshape(top, rows).T
    table = table[jax.random.permutation(jax.random.fold_in(own, 1), rows)]
    offset_by = jax.random.randint(jax.random.fold_in(own, 2), (rows, 1), 0, top)
    return jnp.take_along_axis(table, (jnp.arange(top)[None, :] + offset_by) % top, axis=1)


def shares(count, total, reach, slope, full):
    portions = [(1 << 20) // math.isqrt(rank ** slope) + 1 for rank in range(1, count + 1)]
    largest = reach if full else min(reach, max(-(-total // count), total * portions[0] // sum(portions)))
    least = 1 if total - largest >= count - 1 else 0
    holding, spare = [largest] + [least] * (count - 1), total - largest - least * (count - 1)
    while spare > 0:
        movable = [i for i in range(1, count) if holding[i] < largest] or [i for i in range(1, count) if holding[i] < reach]
        whole, left = sum([portions[i] for i in movable]), spare
        for i in movable:
            more = min(reach - holding[i], max(1, left * portions[i] // whole), spare)
            holding[i] = holding[i] + more
            spare = spare - more
    return np.array(holding)


def normal_values(key, dims, scale, most, shards=(), kind=jnp.bfloat16):
    result = scale * jax.random.normal(key, dims, jnp.float32)
    if shards:
        result = result * block_scale(key, dims, shards, -0.22, 0.18)
    return jnp.clip(result, -most, most).astype(kind)


def setup_inputs(seed: int = 0) -> dict:
    streams_of = jax.random.split(jax.random.key(seed), 10)
    row_block_keys = jax.random.split(jax.random.fold_in(streams_of[0], 1), ROWS // ROW_DEV)
    row_block_turns = jax.random.permutation(jax.random.fold_in(streams_of[0], 3), ROWS // ROW_DEV)
    row_block = jax.vmap(lambda own, number: routed_block(jax.random.fold_in(streams_of[0], 2), own, number, ROW_DEV, NBLK, 1, CAP, 2))(row_block_keys, row_block_turns).reshape((ROWS, 1))
    row_hits = with_ends(jax.random.randint(streams_of[1], (2, ROWS), 0, MODS), jax.random.fold_in(streams_of[1], 1), 0, MODS - 1).astype(jnp.int32)
    row_slot = with_ends(jax.random.randint(streams_of[2], (ROWS,), 0, NB), jax.random.fold_in(streams_of[2], 1), 0, NB - 1).astype(jnp.int32)
    track_kept = with_ends((jax.random.randint(streams_of[3], (TRACKS,), 0, 4) < 3).astype(jnp.int32), jax.random.fold_in(streams_of[3], 1), 0, 1)
    row_derivs = normal_values(streams_of[4], (2 * PAR, ROWS), 0.125, 0.75, ((1, 32),))
    row_resid = normal_values(streams_of[5], (ROWS,), 1.0, 6.0, ((0, 32),))
    row_invsig = jnp.clip(jnp.exp(math.log(2.0) - 1.3862944 * jax.random.uniform(streams_of[6], (ROWS,), jnp.float32) ** block_scale(streams_of[6], (ROWS,), ((0, 32),), -0.2, 0.2)), 0.5, 2.0).astype(jnp.bfloat16)
    pattern = draw_pattern(jax.random.fold_in(streams_of[9], 71), 0)
    prior = draw_prior(jax.random.fold_in(streams_of[9], 71), 0)
    return dict(row_block=row_block, row_hits=row_hits, row_slot=row_slot, track_kept=track_kept, row_derivs=row_derivs, row_resid=row_resid, row_invsig=row_invsig, pattern=pattern, prior=prior)


epsilon = 1e-06

def rounded(value):
    return lax.optimization_barrier(value.astype(jnp.bfloat16)).astype(jnp.float32)

def project(initial_norm, diag_terms, off_terms, basis_list):
    size_count = len(diag_terms)
    zero_value = diag_terms[0] * 0.0
    rows_list = []
    for row_index in range(size_count + 1):
        entries = []
        for column in range(size_count):
            if row_index == column:
                entries.append(diag_terms[column])
            elif row_index == column + 1:
                entries.append(off_terms[column])
            elif column == row_index + 1:
                entries.append(off_terms[row_index])
            else:
                entries.append(zero_value)
        rows_list.append(jnp.stack(entries))
    tridiagonal = jnp.stack(rows_list)
    gram_matrix = jnp.dot(tridiagonal.T, tridiagonal, precision=lax.Precision.HIGHEST)
    target = initial_norm * tridiagonal[0]
    factor = jnp.linalg.cholesky(gram_matrix)
    forward = []
    for row_index in range(size_count):
        partial_sum = target[row_index]
        for column in range(row_index):
            partial_sum = partial_sum - factor[row_index, column] * forward[column]
        forward.append(partial_sum / factor[row_index, row_index])
    backward = [zero_value] * size_count
    for row_index in reversed(range(size_count)):
        partial_sum = forward[row_index]
        for column in range(row_index + 1, size_count):
            partial_sum = partial_sum - factor[column, row_index] * backward[column]
        backward[row_index] = partial_sum / factor[row_index, row_index]
    solution = backward[0] * basis_list[0]
    for row_index in range(1, size_count):
        solution = solution + backward[row_index] * basis_list[row_index]
    return solution

def reference(row_block, row_hits, row_slot, track_kept, row_derivs, row_resid, row_invsig, pattern, prior):
    kept_rows = jnp.repeat(track_kept, SEG).astype(jnp.float32)
    scaling = kept_rows * row_invsig.astype(jnp.float32)
    scaled = rounded(scaling[None, :] * row_derivs.astype(jnp.float32))
    weighted = rounded(scaling * row_resid.astype(jnp.float32))
    first_block = row_block[:, 0].astype(jnp.int32)
    second_block = pattern[first_block, row_slot].astype(jnp.int32)
    first_module = (first_block * MODS + row_hits[0]).astype(jnp.int32)
    second_module = (second_block * MODS + row_hits[1]).astype(jnp.int32)
    first_der = scaled[:PAR].T
    second_der = scaled[PAR:].T
    module_count = NBLK * MODS

    def spread(first_values, second_values):
        summed = jax.ops.segment_sum(first_values, first_module, num_segments=module_count)
        summed = summed + jax.ops.segment_sum(second_values, second_module, num_segments=module_count)
        return summed.reshape(NBLK, ORDER)

    def operate(vector_in):
        flat_field = vector_in.reshape(module_count, PAR)
        along_row = lax.optimization_barrier(jnp.sum(first_der * flat_field[first_module], axis=1))
        along_row = along_row + lax.optimization_barrier(jnp.sum(second_der * flat_field[second_module], axis=1))
        return prior * vector_in + spread(first_der * along_row[:, None], second_der * along_row[:, None])
    gradient = spread(first_der * weighted[:, None], second_der * weighted[:, None])
    initial_norm = jnp.sqrt(jnp.sum(gradient * gradient) + epsilon)
    current = gradient / initial_norm
    previous = jnp.zeros_like(gradient)
    beta_term = jnp.zeros((), jnp.float32)
    diag_terms, off_terms, basis_list = ([], [], [])
    for iteration in range(ITERS):
        image_vec = operate(current)
        alpha_term = jnp.sum(current * image_vec)
        direction = image_vec - alpha_term * current - beta_term * previous
        beta_next = jnp.sqrt(jnp.sum(direction * direction) + epsilon)
        diag_terms.append(alpha_term)
        off_terms.append(beta_next)
        basis_list.append(current)
        previous, current, beta_term = (current, direction / beta_next, beta_next)
    solution = project(initial_norm, diag_terms, off_terms, basis_list)
    return (solution, gradient)
```

```python
import functools

import jax
import jax.numpy as jnp
from jax import lax
from jax.experimental import pallas as pl
from jax.experimental.pallas import tpu as pltpu
from jax.sharding import PartitionSpec as P

MODS = 64
PAR = 6
NB = 5
SEG = 8
ITERS = 2


epsilon = 1e-06


def passed_along(block, axis, distance):
    devices = range(lax.axis_size(axis))
    route = [((i - distance) % len(devices), i) for i in devices]
    return lax.ppermute(block, axis, route)


def project(initial_norm, diag_terms, off_terms, basis_list):
    size_count = len(diag_terms)
    zero_value = diag_terms[0] * 0.0
    rows_list = []
    for row_index in range(size_count + 1):
        entries = []
        for column in range(size_count):
            if row_index == column:
                entries.append(diag_terms[column])
            elif row_index == column + 1:
                entries.append(off_terms[column])
            elif column == row_index + 1:
                entries.append(off_terms[row_index])
            else:
                entries.append(zero_value)
        rows_list.append(jnp.stack(entries))
    tridiagonal = jnp.stack(rows_list)
    gram_matrix = jnp.dot(tridiagonal.T, tridiagonal, precision=lax.Precision.HIGHEST)
    target = initial_norm * tridiagonal[0]
    factor = jnp.linalg.cholesky(gram_matrix)
    forward = []
    for row_index in range(size_count):
        partial_sum = target[row_index]
        for column in range(row_index):
            partial_sum = partial_sum - factor[row_index, column] * forward[column]
        forward.append(partial_sum / factor[row_index, row_index])
    backward = [zero_value] * size_count
    for row_index in reversed(range(size_count)):
        partial_sum = forward[row_index]
        for column in range(row_index + 1, size_count):
            partial_sum = partial_sum - factor[column, row_index] * backward[column]
        backward[row_index] = partial_sum / factor[row_index, row_index]
    solution = backward[0] * basis_list[0]
    row_index = 1
    solution = solution + backward[row_index] * basis_list[row_index]
    return solution


def contract(left_rows, right_rows):
    return lax.dot_general(
        left_rows, right_rows, (((0,), (0,)), ((), ())), preferred_element_type=jnp.float32
    )


def on_device_large(
    row_block, row_hits, row_slot, track_kept, row_derivs, row_resid, row_invsig, pattern, prior
):
    row_count = row_resid.shape[0]
    owners = lax.axis_size("blk")
    capacity = 2 * row_count // owners
    order_size = MODS * PAR
    kept_rows = jnp.repeat(track_kept, SEG).astype(jnp.float32)
    scaling = kept_rows * row_invsig.astype(jnp.float32)
    scaled = (scaling[None, :] * row_derivs.astype(jnp.float32)).astype(jnp.bfloat16)
    weighted = (scaling * row_resid.astype(jnp.float32)).astype(jnp.bfloat16)
    destination = row_block[:, 0]
    member = (destination[:, None] == jnp.arange(owners, dtype=jnp.int32)[None, :]).astype(
        jnp.bfloat16
    )
    row_ids = jnp.arange(row_count, dtype=jnp.int32)
    earlier = (row_ids[:, None] > row_ids[None, :]).astype(jnp.bfloat16)
    before = jnp.dot(earlier, member, preferred_element_type=jnp.float32)
    rank_within = jnp.sum(before * member.astype(jnp.float32), axis=1).astype(jnp.int32)
    slot_place = destination * capacity + rank_within
    labels = jnp.stack([row_hits[0], row_hits[1], row_slot]).astype(jnp.bfloat16)
    record = jnp.concatenate([scaled, weighted[None, :], labels], axis=0)
    outgoing = (
        jnp.zeros((record.shape[0], owners * capacity), jnp.bfloat16).at[:, slot_place].set(record)
    )
    incoming = lax.all_to_all(outgoing, "blk", split_axis=1, concat_axis=1, tiled=True)
    column_ids = jnp.arange(order_size, dtype=jnp.int32)
    column_module = column_ids // PAR
    column_param = column_ids % PAR

    def expand(values, module_ids):
        spread = jnp.zeros((values.shape[1], order_size), jnp.bfloat16)
        for component in range(PAR):
            spread = jnp.where(
                column_param[None, :] == component, values[component][:, None], spread
            )
        return jnp.where(
            module_ids[:, None] == column_module[None, :], spread, jnp.zeros_like(spread)
        )

    first_module = incoming[2 * PAR + 1].astype(jnp.int32)
    second_module = incoming[2 * PAR + 2].astype(jnp.int32)
    slot_in = incoming[2 * PAR + 3].astype(jnp.int32)
    resid_in = incoming[2 * PAR]
    first_rows = expand(incoming[0:PAR], first_module)
    second_rows = expand(incoming[PAR : 2 * PAR], second_module)
    own_block = contract(first_rows, first_rows)
    grad_own = jnp.dot(resid_in, first_rows, preferred_element_type=jnp.float32)
    cross_list, partner_list, grad_list = ([], [], [])
    for slot_id in range(NB):
        masked = jnp.where((slot_in == slot_id)[:, None], second_rows, jnp.zeros_like(second_rows))
        cross_list.append(contract(first_rows, masked))
        partner_list.append(contract(masked, masked))
        grad_list.append(jnp.dot(resid_in, masked, preferred_element_type=jnp.float32))
    cross_blocks = jnp.stack(cross_list)
    partner_blocks = jnp.stack(partner_list)
    grad_partner = jnp.stack(grad_list)
    position = lax.axis_index("blk")
    neighbours = pattern[0]
    offset = (neighbours - position) % owners
    offset = jnp.where(offset > owners // 2, offset - owners, offset)

    def deliver(own_term, partner_terms):
        local_sum = own_term + jnp.sum(
            jnp.where((offset == 0)[:, None], partner_terms, 0.0), axis=0, keepdims=True
        )
        for shift_by in (-2, -1, 1, 2):
            sending = jnp.sum(
                jnp.where((offset == shift_by)[:, None], partner_terms, 0.0), axis=0, keepdims=True
            )
            local_sum = local_sum + passed_along(sending, "blk", shift_by)
        return lax.psum(local_sum, "trk")

    gradient = deliver(grad_own[None, :], grad_partner)
    initial_norm = jnp.sqrt(lax.psum(jnp.sum(gradient * gradient), "blk") + epsilon)
    current = gradient / initial_norm
    previous = jnp.zeros_like(gradient)
    beta_term = jnp.zeros((), jnp.float32)
    diag_terms, off_terms, basis_list = ([], [], [])
    for iteration in range(ITERS):
        result = jnp.where((offset == 0)[:, None], current, 0.0)
        for fetch_shift_by in (-2, -1, 1, 2):
            arrived = passed_along(current, "blk", -fetch_shift_by)
            result = result + jnp.where((offset == fetch_shift_by)[:, None], arrived, 0.0)
        operate_own_term = jnp.dot(own_block, current[0], precision=lax.Precision.HIGHEST)
        operate_own_term = operate_own_term + jnp.einsum(
            "kij,kj->i", cross_blocks, result, precision=lax.Precision.HIGHEST
        )
        operate_partner_terms = jnp.einsum(
            "kij,i->kj", cross_blocks, current[0], precision=lax.Precision.HIGHEST
        )
        operate_partner_terms = operate_partner_terms + jnp.einsum(
            "kij,kj->ki", partner_blocks, result, precision=lax.Precision.HIGHEST
        )
        image_vec = prior * current + deliver(operate_own_term[None, :], operate_partner_terms)
        alpha_term = lax.psum(jnp.sum(current * image_vec), "blk")
        direction = image_vec - alpha_term * current - beta_term * previous
        beta_next = jnp.sqrt(lax.psum(jnp.sum(direction * direction), "blk") + epsilon)
        diag_terms.append(alpha_term)
        off_terms.append(beta_next)
        basis_list.append(current)
        previous, current, beta_term = (current, direction / beta_next, beta_next)
    solution = project(initial_norm, diag_terms, off_terms, basis_list)
    return (solution, gradient)


LANES = 128
WIDE = 8
PHASES = ITERS + 1
RECORD = 16
EXTRA = 3
MESH = pl.DeviceIdType.MESH


def three_parts(value):
    high = value.astype(jnp.bfloat16).astype(jnp.float32)
    rest = value - high
    middle = rest.astype(jnp.bfloat16).astype(jnp.float32)
    return jnp.concatenate([high, middle, rest - middle], axis=0).astype(jnp.bfloat16)


def two_parts(value, axis):
    high = value.astype(jnp.bfloat16)
    low = (value - high.astype(jnp.float32)).astype(jnp.bfloat16)
    return jnp.concatenate([high, low], axis=axis)


def total(value):
    return jnp.sum(jnp.sum(value, axis=0, keepdims=True), axis=1, keepdims=True)


def onehot(mask):
    return mask.astype(jnp.float32).astype(jnp.bfloat16)


def kernel(
    owners,
    shares,
    block_ref,
    hits_ref,
    slot_ref,
    kept_ref,
    derivs_ref,
    resid_ref,
    invsig_ref,
    pattern_ref,
    prior_ref,
    out_ref,
    block_in,
    hits_in,
    slot_in,
    kept_in,
    derivs_in,
    resid_in,
    invsig_in,
    pattern_in,
    prior_in,
    input_sem,
    record,
    extra,
    spread,
    labels,
    grads,
    mine,
    other,
    record_send,
    record_recv,
    extra_send,
    extra_recv,
    swap_send,
    swap_recv,
):
    blk, trk = lax.axis_index("blk"), lax.axis_index("trk")
    rows = block_ref.shape[1]
    tracks = kept_ref.shape[1]
    pairs = shares // 2
    pair, half = trk // 2, lax.rem(trk, 2)
    sibling = {"blk": blk, "trk": pair * 2 + 1 - half}
    order_size = MODS * PAR
    portion = order_size // shares

    def peer(c, j):
        return {"blk": lax.rem(blk + c, owners), "trk": lax.rem(pair + j, pairs) * 2 + half}

    steps = [(c, j) for c in range(owners) for j in range(pairs) if c or j]
    far_first = sorted(steps, key=lambda step: (abs(step[0] - owners // 2), -step[1]))
    barrier = pltpu.get_barrier_semaphore()
    for target in [peer(c, j) for c, j in far_first] + [sibling]:
        pl.semaphore_signal(barrier, inc=1, device_id=target, device_id_type=MESH)

    outside = (
        kept_ref, invsig_ref, derivs_ref, resid_ref, block_ref, hits_ref, slot_ref, prior_ref, pattern_ref
    )
    inside = (
        kept_in, invsig_in, derivs_in, resid_in, block_in, hits_in, slot_in, prior_in, pattern_in
    )
    fetches = [
        pltpu.make_async_copy(source, target, input_sem.at[i])
        for i, (source, target) in enumerate(zip(outside, inside))
    ]
    for one in fetches:
        one.start()
    for one in fetches:
        one.wait()

    def copy(source, target, send, recv, device):
        return pltpu.make_async_remote_copy(
            src_ref=source, dst_ref=target, send_sem=send, recv_sem=recv, device_id=device, device_id_type=MESH
        )

    track_of = lax.broadcasted_iota(jnp.int32, (tracks, rows), 1) // SEG
    track_id = lax.broadcasted_iota(jnp.int32, (tracks, rows), 0)
    kept_rows = jnp.dot(
        onehot(jnp.broadcast_to(kept_in[...], (WIDE, tracks)) > 0),
        onehot(track_of == track_id),
        preferred_element_type=jnp.float32,
    )[0:1]
    scaling = kept_rows * invsig_in[...].reshape(1, rows).astype(jnp.float32)
    scaled = scaling * derivs_in[...].astype(jnp.float32)
    weighted = scaling * resid_in[...].reshape(1, rows).astype(jnp.float32)
    record[blk, pair] = jnp.concatenate(
        [scaled, weighted, hits_in[...].astype(jnp.float32), slot_in[...].astype(jnp.float32)], axis=0
    ).astype(jnp.bfloat16)
    block_row = block_in[...].astype(jnp.float32)
    for piece in range(rows // LANES):
        extra[blk, pair, piece : piece + 1] = block_row[:, piece * LANES : (piece + 1) * LANES]
    last = rows // LANES
    own = jnp.zeros((1, portion), jnp.float32)
    for t in range(shares):
        own = jnp.where(trk == t, prior_in[:, t * portion : (t + 1) * portion], own)
    extra[blk, pair, last : last + 1, 0:portion] = own
    extra[blk, pair, last : last + 1, portion : portion + NB] = pattern_in[...].astype(jnp.float32)

    pl.semaphore_wait(barrier, len(steps) + 1)
    extras = {
        (c, j): copy(
            extra.at[blk, pair], extra.at[blk, pair], extra_send.at[c, j], extra_recv.at[c, j], peer(c, j)
        )
        for c, j in far_first
    }
    records = {
        (c, j): copy(
            record.at[blk, pair], record.at[blk, pair], record_send.at[c, j], record_recv.at[c, j], peer(c, j)
        )
        for c, j in far_first
    }
    for step in far_first:
        extras[step].start()
    for step in far_first:
        records[step].start()

    block_ids = lax.broadcasted_iota(jnp.int32, (WIDE, rows), 0).astype(jnp.float32)
    module_ids = lax.broadcasted_iota(jnp.int32, (MODS, 2 * rows), 0).astype(jnp.float32)
    for step in far_first:
        extras[step].wait_recv()
    side = [extra[:, j, last, :] for j in range(pairs)]
    columns = [
        jnp.broadcast_to(side[0][:, portion + s : portion + s + 1], (WIDE, rows)) for s in range(NB)
    ]

    near_first = [(0, 0)] + far_first[::-1]
    for c, j in near_first:
        if c or j:
            records[(c, j)].wait_recv()
        b, p = lax.rem(blk + owners - c, owners), lax.rem(pair + pairs - j, pairs)
        values = record[b, p].astype(jnp.float32)
        first_block = jnp.concatenate([extra[b, p, i : i + 1] for i in range(last)], axis=1)
        first = block_ids == first_block
        slot = values[2 * PAR + 3 : 2 * PAR + 4]
        coupled = columns[0]
        for s in range(1, NB):
            coupled = jnp.where(slot == s, columns[s], coupled)
        second_block = jnp.sum(jnp.where(first, coupled, 0.0), axis=0, keepdims=True)
        second = block_ids == second_block
        terms = []
        for i in range(PAR):
            terms.append(
                jnp.concatenate(
                    [
                        jnp.where(first, values[i : i + 1], 0.0),
                        jnp.where(second, values[PAR + i : PAR + i + 1], 0.0),
                    ],
                    axis=1,
                )
            )
        terms = jnp.concatenate(terms, axis=0)
        spread[b, p] = terms
        hits = jnp.concatenate(
            [values[2 * PAR + 1 : 2 * PAR + 2], values[2 * PAR + 2 : 2 * PAR + 3]], axis=1
        )
        named = onehot(module_ids == hits)
        labels[b, p, 0:MODS] = named
        labels[b, p, MODS : 2 * MODS] = named
        weight = values[2 * PAR : 2 * PAR + 1]
        grads[b, p] = scatter(terms * jnp.concatenate([weight, weight], axis=1), named)

    def add_up(phase, value):
        mine[phase] = value
        swap = copy(mine.at[phase], other.at[phase], swap_send.at[phase], swap_recv.at[phase], sibling)
        swap.start()
        swap.wait_recv()
        swaps.append(swap)
        return value + other[phase]

    swaps = []
    gradient = grads[0, 0]
    for k in range(1, owners * pairs):
        gradient = gradient + grads[k // pairs, k % pairs]
    gradient = add_up(0, gradient)

    lane = lax.broadcasted_iota(jnp.int32, (LANES, order_size), 0)
    column = lax.broadcasted_iota(jnp.int32, (LANES, order_size), 1)
    prior = jnp.zeros((WIDE, order_size), jnp.float32)
    for j in range(pairs):
        module = lane // PAR + (2 * j + half) * (portion // PAR)
        place = onehot(
            (lane < portion) & (column == lax.rem(lane, PAR) * MODS + module)
        )
        laid = jnp.dot(three_parts(side[j]), place, preferred_element_type=jnp.float32)
        prior = prior + (laid[0:WIDE] + laid[WIDE : 2 * WIDE] + laid[2 * WIDE :])
    prior = jnp.concatenate([prior[:, i * MODS : (i + 1) * MODS] for i in range(PAR)], axis=0)

    def matvec(vector):
        parts = two_parts(vector, 1)
        summed = jnp.zeros((PAR * WIDE, MODS), jnp.float32)
        for k in range(owners * pairs):
            b, p = k // pairs, k % pairs
            terms = spread[b, p]
            read = jnp.dot(parts, labels[b, p], preferred_element_type=jnp.float32)
            along = jnp.sum(terms * read, axis=0, keepdims=True)
            along = along[:, 0:rows] + along[:, rows : 2 * rows]
            summed = summed + scatter(terms * jnp.concatenate([along, along], axis=1), labels[b, p, 0:MODS])
        return summed + prior * vector

    initial_norm = jnp.sqrt(total(gradient * gradient) + epsilon)
    current = gradient / initial_norm
    previous = jnp.zeros_like(gradient)
    beta_term = jnp.zeros((1, 1), jnp.float32)
    diag_terms, off_terms, basis_list = ([], [], [])
    for iteration in range(ITERS):
        image_vec = add_up(iteration + 1, matvec(current))
        alpha_term = total(current * image_vec)
        direction = image_vec - alpha_term * current - beta_term * previous
        beta_next = jnp.sqrt(total(direction * direction) + epsilon)
        diag_terms.append(alpha_term)
        off_terms.append(beta_next)
        basis_list.append(current)
        previous, current, beta_term = (current, direction / beta_next, beta_next)

    module_row = lax.broadcasted_iota(jnp.int32, (MODS, order_size), 0)
    module_of = lax.broadcasted_iota(jnp.int32, (MODS, order_size), 1) // PAR
    place = onehot(module_row == module_of)
    component = lax.broadcasted_iota(jnp.int32, (WIDE, order_size), 0)
    parameter = lax.broadcasted_iota(jnp.int32, (WIDE, order_size), 1)
    own_entry = component == lax.rem(parameter, PAR)
    own_block = lax.broadcasted_iota(jnp.int32, (WIDE, MODS), 0) == blk

    def in_order(vector):
        own = [
            jnp.sum(jnp.where(own_block, vector[i * WIDE : (i + 1) * WIDE], 0.0), axis=0, keepdims=True)
            for i in range(PAR)
        ]
        own = jnp.concatenate(own + [jnp.zeros((WIDE - PAR, MODS), jnp.float32)], axis=0)
        laid = jnp.dot(three_parts(own), place, preferred_element_type=jnp.float32)
        laid = laid[0:WIDE] + laid[WIDE : 2 * WIDE] + laid[2 * WIDE :]
        return jnp.sum(jnp.where(own_entry, laid, 0.0), axis=0, keepdims=True)

    out_ref[1:2] = in_order(gradient)

    first, second = diag_terms
    below, last_term = off_terms
    corner = first * first + below * below
    side_term = first * below + below * second
    end = below * below + second * second + last_term * last_term
    root = jnp.sqrt(corner)
    lower = side_term / root
    tip = jnp.sqrt(end - lower * lower)
    forward = initial_norm * first / root
    forward_next = (initial_norm * below - lower * forward) / tip
    back_next = forward_next / tip
    back = (forward - lower * back_next) / root
    result = back * basis_list[0] + back_next * basis_list[1]
    out_ref[0:1] = in_order(result)
    for one in list(extras.values()) + list(records.values()) + swaps:
        one.wait_send()


def scatter(values, named):
    summed = lax.dot_general(
        two_parts(values, 0), named, (((1,), (1,)), ((), ())), preferred_element_type=jnp.float32
    )
    return summed[0 : PAR * WIDE] + summed[PAR * WIDE :]


def on_device(
    row_block,
    row_hits,
    row_slot,
    track_kept,
    row_derivs,
    row_resid,
    row_invsig,
    pattern,
    prior,
    owners,
    shares,
):
    args = (
        row_block, row_hits, row_slot, track_kept, row_derivs, row_resid, row_invsig, pattern, prior
    )
    if owners != WIDE or shares % 2 or MODS % shares:
        return on_device_large(*args)
    rows = row_resid.shape[0]
    dma = pltpu.SemaphoreType.DMA
    pairs = shares // 2
    vector = (PAR * WIDE, MODS)
    out = pl.pallas_call(
        functools.partial(kernel, owners, shares),
        out_shape=jax.ShapeDtypeStruct((2, MODS * PAR), jnp.float32),
        in_specs=[pl.BlockSpec(memory_space=pltpu.HBM)] * 9,
        out_specs=pl.BlockSpec(memory_space=pltpu.VMEM),
        scratch_shapes=[
            pltpu.VMEM((1, rows), jnp.int32),
            pltpu.VMEM((2, rows), jnp.int32),
            pltpu.VMEM((1, rows), jnp.int32),
            pltpu.VMEM((1, track_kept.shape[0]), jnp.int32),
            pltpu.VMEM((2 * PAR, rows), jnp.bfloat16),
            pltpu.VMEM((rows,), jnp.bfloat16),
            pltpu.VMEM((rows,), jnp.bfloat16),
            pltpu.VMEM((1, NB), jnp.int32),
            pltpu.VMEM((1, MODS * PAR), jnp.float32),
            dma((9,)),
            pltpu.VMEM((owners, pairs, RECORD, rows), jnp.bfloat16),
            pltpu.VMEM((owners, pairs, EXTRA, LANES), jnp.float32),
            pltpu.VMEM((owners, pairs, PAR * WIDE, 2 * rows), jnp.float32),
            pltpu.VMEM((owners, pairs, 2 * MODS, 2 * rows), jnp.bfloat16),
            pltpu.VMEM((owners, pairs) + vector, jnp.float32),
            pltpu.VMEM((PHASES,) + vector, jnp.float32),
            pltpu.VMEM((PHASES,) + vector, jnp.float32),
            dma((owners, pairs)),
            dma((owners, pairs)),
            dma((owners, pairs)),
            dma((owners, pairs)),
            dma((PHASES,)),
            dma((PHASES,)),
        ],
        compiler_params=pltpu.CompilerParams(
            collective_id=0, has_side_effects=True, vmem_limit_bytes=60 * 1024 * 1024
        ),
    )(
        row_block.reshape(1, rows),
        row_hits,
        row_slot.reshape(1, rows),
        track_kept.reshape(1, -1),
        row_derivs,
        row_resid,
        row_invsig,
        pattern,
        prior,
    )
    return out[0:1], out[1:2]


def solution(mesh):
    return jax.shard_map(
        functools.partial(on_device, owners=mesh.shape["blk"], shares=mesh.shape["trk"]),
        mesh=mesh,
        in_specs=(
            P(("blk", "trk"), None),
            P(None, ("blk", "trk")),
            P(("blk", "trk")),
            P(("blk", "trk")),
            P(None, ("blk", "trk")),
            P(("blk", "trk")),
            P(("blk", "trk")),
            P("blk", None),
            P("blk", None),
        ),
        out_specs=(P("blk", None), P("blk", None)),
        check_vma=False,
    )
```

```python
import functools

import jax
import jax.numpy as jnp
from jax import lax
from jax.experimental import pallas as pl
from jax.experimental.pallas import tpu as pltpu
from jax.sharding import PartitionSpec as P

MODS = 64
PAR = 6
NB = 5
SEG = 8
ITERS = 2


epsilon = 1e-06


def passed_along(block, axis, distance):
    devices = range(lax.axis_size(axis))
    route = [((i - distance) % len(devices), i) for i in devices]
    return lax.ppermute(block, axis, route)


def project(initial_norm, diag_terms, off_terms, basis_list):
    size_count = len(diag_terms)
    zero_value = diag_terms[0] * 0.0
    rows_list = []
    for row_index in range(size_count + 1):
        entries = []
        for column in range(size_count):
            if row_index == column:
                entries.append(diag_terms[column])
            elif row_index == column + 1:
                entries.append(off_terms[column])
            elif column == row_index + 1:
                entries.append(off_terms[row_index])
            else:
                entries.append(zero_value)
        rows_list.append(jnp.stack(entries))
    tridiagonal = jnp.stack(rows_list)
    gram_matrix = jnp.dot(tridiagonal.T, tridiagonal, precision=lax.Precision.HIGHEST)
    target = initial_norm * tridiagonal[0]
    factor = jnp.linalg.cholesky(gram_matrix)
    forward = []
    for row_index in range(size_count):
        partial_sum = target[row_index]
        for column in range(row_index):
            partial_sum = partial_sum - factor[row_index, column] * forward[column]
        forward.append(partial_sum / factor[row_index, row_index])
    backward = [zero_value] * size_count
    for row_index in reversed(range(size_count)):
        partial_sum = forward[row_index]
        for column in range(row_index + 1, size_count):
            partial_sum = partial_sum - factor[column, row_index] * backward[column]
        backward[row_index] = partial_sum / factor[row_index, row_index]
    solution = backward[0] * basis_list[0]
    row_index = 1
    solution = solution + backward[row_index] * basis_list[row_index]
    return solution


def contract(left_rows, right_rows):
    return lax.dot_general(
        left_rows, right_rows, (((0,), (0,)), ((), ())), preferred_element_type=jnp.float32
    )


def on_device_large(
    row_block, row_hits, row_slot, track_kept, row_derivs, row_resid, row_invsig, pattern, prior
):
    row_count = row_resid.shape[0]
    owners = lax.axis_size("blk")
    capacity = 2 * row_count // owners
    order_size = MODS * PAR
    kept_rows = jnp.repeat(track_kept, SEG).astype(jnp.float32)
    scaling = kept_rows * row_invsig.astype(jnp.float32)
    scaled = (scaling[None, :] * row_derivs.astype(jnp.float32)).astype(jnp.bfloat16)
    weighted = (scaling * row_resid.astype(jnp.float32)).astype(jnp.bfloat16)
    destination = row_block[:, 0]
    member = (destination[:, None] == jnp.arange(owners, dtype=jnp.int32)[None, :]).astype(
        jnp.bfloat16
    )
    row_ids = jnp.arange(row_count, dtype=jnp.int32)
    earlier = (row_ids[:, None] > row_ids[None, :]).astype(jnp.bfloat16)
    before = jnp.dot(earlier, member, preferred_element_type=jnp.float32)
    rank_within = jnp.sum(before * member.astype(jnp.float32), axis=1).astype(jnp.int32)
    slot_place = destination * capacity + rank_within
    labels = jnp.stack([row_hits[0], row_hits[1], row_slot]).astype(jnp.bfloat16)
    record = jnp.concatenate([scaled, weighted[None, :], labels], axis=0)
    outgoing = (
        jnp.zeros((record.shape[0], owners * capacity), jnp.bfloat16).at[:, slot_place].set(record)
    )
    incoming = lax.all_to_all(outgoing, "blk", split_axis=1, concat_axis=1, tiled=True)
    column_ids = jnp.arange(order_size, dtype=jnp.int32)
    column_module = column_ids // PAR
    column_param = column_ids % PAR

    def expand(values, module_ids):
        spread = jnp.zeros((values.shape[1], order_size), jnp.bfloat16)
        for component in range(PAR):
            spread = jnp.where(
                column_param[None, :] == component, values[component][:, None], spread
            )
        return jnp.where(
            module_ids[:, None] == column_module[None, :], spread, jnp.zeros_like(spread)
        )

    first_module = incoming[2 * PAR + 1].astype(jnp.int32)
    second_module = incoming[2 * PAR + 2].astype(jnp.int32)
    slot_in = incoming[2 * PAR + 3].astype(jnp.int32)
    resid_in = incoming[2 * PAR]
    first_rows = expand(incoming[0:PAR], first_module)
    second_rows = expand(incoming[PAR : 2 * PAR], second_module)
    own_block = contract(first_rows, first_rows)
    grad_own = jnp.dot(resid_in, first_rows, preferred_element_type=jnp.float32)
    cross_list, partner_list, grad_list = ([], [], [])
    for slot_id in range(NB):
        masked = jnp.where((slot_in == slot_id)[:, None], second_rows, jnp.zeros_like(second_rows))
        cross_list.append(contract(first_rows, masked))
        partner_list.append(contract(masked, masked))
        grad_list.append(jnp.dot(resid_in, masked, preferred_element_type=jnp.float32))
    cross_blocks = jnp.stack(cross_list)
    partner_blocks = jnp.stack(partner_list)
    grad_partner = jnp.stack(grad_list)
    position = lax.axis_index("blk")
    neighbours = pattern[0]
    offset = (neighbours - position) % owners
    offset = jnp.where(offset > owners // 2, offset - owners, offset)

    def deliver(own_term, partner_terms):
        local_sum = own_term + jnp.sum(
            jnp.where((offset == 0)[:, None], partner_terms, 0.0), axis=0, keepdims=True
        )
        for shift_by in (-2, -1, 1, 2):
            sending = jnp.sum(
                jnp.where((offset == shift_by)[:, None], partner_terms, 0.0), axis=0, keepdims=True
            )
            local_sum = local_sum + passed_along(sending, "blk", shift_by)
        return lax.psum(local_sum, "trk")

    gradient = deliver(grad_own[None, :], grad_partner)
    initial_norm = jnp.sqrt(lax.psum(jnp.sum(gradient * gradient), "blk") + epsilon)
    current = gradient / initial_norm
    previous = jnp.zeros_like(gradient)
    beta_term = jnp.zeros((), jnp.float32)
    diag_terms, off_terms, basis_list = ([], [], [])
    for iteration in range(ITERS):
        result = jnp.where((offset == 0)[:, None], current, 0.0)
        for fetch_shift_by in (-2, -1, 1, 2):
            arrived = passed_along(current, "blk", -fetch_shift_by)
            result = result + jnp.where((offset == fetch_shift_by)[:, None], arrived, 0.0)
        operate_own_term = jnp.dot(own_block, current[0], precision=lax.Precision.HIGHEST)
        operate_own_term = operate_own_term + jnp.einsum(
            "kij,kj->i", cross_blocks, result, precision=lax.Precision.HIGHEST
        )
        operate_partner_terms = jnp.einsum(
            "kij,i->kj", cross_blocks, current[0], precision=lax.Precision.HIGHEST
        )
        operate_partner_terms = operate_partner_terms + jnp.einsum(
            "kij,kj->ki", partner_blocks, result, precision=lax.Precision.HIGHEST
        )
        image_vec = prior * current + deliver(operate_own_term[None, :], operate_partner_terms)
        alpha_term = lax.psum(jnp.sum(current * image_vec), "blk")
        direction = image_vec - alpha_term * current - beta_term * previous
        beta_next = jnp.sqrt(lax.psum(jnp.sum(direction * direction), "blk") + epsilon)
        diag_terms.append(alpha_term)
        off_terms.append(beta_next)
        basis_list.append(current)
        previous, current, beta_term = (current, direction / beta_next, beta_next)
    solution = project(initial_norm, diag_terms, off_terms, basis_list)
    return (solution, gradient)


LANES = 128
WIDE = 8
PHASES = ITERS + 1
RECORD = 16
EXTRA = 3
MESH = pl.DeviceIdType.MESH


def three_parts(value):
    high = value.astype(jnp.bfloat16).astype(jnp.float32)
    rest = value - high
    middle = rest.astype(jnp.bfloat16).astype(jnp.float32)
    return jnp.concatenate([high, middle, rest - middle], axis=0).astype(jnp.bfloat16)


def two_parts(value, axis):
    high = value.astype(jnp.bfloat16)
    low = (value - high.astype(jnp.float32)).astype(jnp.bfloat16)
    return jnp.concatenate([high, low], axis=axis)


def total(value):
    return jnp.sum(jnp.sum(value, axis=0, keepdims=True), axis=1, keepdims=True)


def onehot(mask):
    return mask.astype(jnp.float32).astype(jnp.bfloat16)


def kernel(
    owners,
    shares,
    block_ref,
    hits_ref,
    slot_ref,
    kept_ref,
    derivs_ref,
    resid_ref,
    invsig_ref,
    pattern_ref,
    prior_ref,
    out_ref,
    block_in,
    hits_in,
    slot_in,
    kept_in,
    derivs_in,
    resid_in,
    invsig_in,
    pattern_in,
    prior_in,
    input_sem,
    record,
    extra,
    spread,
    labels,
    turned,
    products,
    mine,
    other,
    record_send,
    record_recv,
    extra_send,
    extra_recv,
    swap_send,
    swap_recv,
):
    blk, trk = lax.axis_index("blk"), lax.axis_index("trk")
    rows = block_ref.shape[1]
    tracks = kept_ref.shape[1]
    pairs = shares // 2
    pair, half = trk // 2, lax.rem(trk, 2)
    sibling = {"blk": blk, "trk": pair * 2 + 1 - half}
    order_size = MODS * PAR
    portion = order_size // shares

    def peer(c, j):
        return {"blk": lax.rem(blk + c, owners), "trk": lax.rem(pair + j, pairs) * 2 + half}

    steps = [(c, j) for c in range(owners) for j in range(pairs) if c or j]
    far_first = sorted(steps, key=lambda step: (abs(step[0] - owners // 2), -step[1]))
    barrier = pltpu.get_barrier_semaphore()
    for target in [peer(c, j) for c, j in far_first] + [sibling]:
        pl.semaphore_signal(barrier, inc=1, device_id=target, device_id_type=MESH)

    outside = (
        kept_ref, invsig_ref, derivs_ref, resid_ref, block_ref, hits_ref, slot_ref, prior_ref, pattern_ref
    )
    inside = (
        kept_in, invsig_in, derivs_in, resid_in, block_in, hits_in, slot_in, prior_in, pattern_in
    )
    fetches = [
        pltpu.make_async_copy(source, target, input_sem.at[i])
        for i, (source, target) in enumerate(zip(outside, inside))
    ]
    for one in fetches:
        one.start()
    for one in fetches:
        one.wait()

    def copy(source, target, send, recv, device):
        return pltpu.make_async_remote_copy(
            src_ref=source, dst_ref=target, send_sem=send, recv_sem=recv, device_id=device, device_id_type=MESH
        )

    track_of = lax.broadcasted_iota(jnp.int32, (tracks, rows), 1) // SEG
    track_id = lax.broadcasted_iota(jnp.int32, (tracks, rows), 0)
    kept_rows = jnp.dot(
        onehot(jnp.broadcast_to(kept_in[...], (WIDE, tracks)) > 0),
        onehot(track_of == track_id),
        preferred_element_type=jnp.float32,
    )[0:1]
    scaling = kept_rows * invsig_in[...].reshape(1, rows).astype(jnp.float32)
    scaled = scaling * derivs_in[...].astype(jnp.float32)
    weighted = scaling * resid_in[...].reshape(1, rows).astype(jnp.float32)
    record[blk, pair] = jnp.concatenate(
        [scaled, weighted, hits_in[...].astype(jnp.float32), slot_in[...].astype(jnp.float32)], axis=0
    ).astype(jnp.bfloat16)
    block_row = block_in[...].astype(jnp.float32)
    for piece in range(rows // LANES):
        extra[blk, pair, piece : piece + 1] = block_row[:, piece * LANES : (piece + 1) * LANES]
    last = rows // LANES
    own = jnp.zeros((1, portion), jnp.float32)
    for t in range(shares):
        own = jnp.where(trk == t, prior_in[:, t * portion : (t + 1) * portion], own)
    extra[blk, pair, last : last + 1, 0:portion] = own
    extra[blk, pair, last : last + 1, portion : portion + NB] = pattern_in[...].astype(jnp.float32)

    pl.semaphore_wait(barrier, len(steps) + 1)
    extras = {
        (c, j): copy(
            extra.at[blk, pair], extra.at[blk, pair], extra_send.at[c, j], extra_recv.at[c, j], peer(c, j)
        )
        for c, j in far_first
    }
    records = {
        (c, j): copy(
            record.at[blk, pair], record.at[blk, pair], record_send.at[c, j], record_recv.at[c, j], peer(c, j)
        )
        for c, j in far_first
    }
    for step in far_first:
        extras[step].start()
    for step in far_first:
        records[step].start()

    size = PAR * WIDE
    block_ids = lax.broadcasted_iota(jnp.int32, (WIDE, rows), 0).astype(jnp.float32)
    lane_ids = lax.broadcasted_iota(jnp.int32, (rows, LANES), 1).astype(jnp.float32)
    module_ids = lax.broadcasted_iota(jnp.int32, (MODS, 2 * rows), 0).astype(jnp.float32)
    for step in far_first:
        extras[step].wait_recv()
    side = [extra[:, j, last, :] for j in range(pairs)]
    columns = [
        jnp.broadcast_to(side[0][:, portion + s : portion + s + 1], (WIDE, rows)) for s in range(NB)
    ]

    def prepare(b, p):
        values = record[b, p].astype(jnp.float32)
        first_block = jnp.concatenate([extra[b, p, i : i + 1] for i in range(last)], axis=1)
        first = block_ids == first_block
        slot = values[2 * PAR + 3 : 2 * PAR + 4]
        coupled = columns[0]
        for s in range(1, NB):
            coupled = jnp.where(slot == s, columns[s], coupled)
        second_block = jnp.sum(jnp.where(first, coupled, 0.0), axis=0, keepdims=True)
        second = block_ids == second_block
        terms = []
        for i in range(PAR):
            terms.append(
                jnp.concatenate(
                    [
                        jnp.where(first, values[i : i + 1], 0.0),
                        jnp.where(second, values[PAR + i : PAR + i + 1], 0.0),
                    ],
                    axis=1,
                )
            )
        terms = jnp.concatenate(terms, axis=0)
        spread[b, p] = terms
        upright = jnp.transpose(values)
        upright = onehot(
            jnp.concatenate(
                [
                    lane_ids == upright[:, 2 * PAR + 1 : 2 * PAR + 2],
                    lane_ids == upright[:, 2 * PAR + 2 : 2 * PAR + 3],
                ],
                axis=0,
            )
        )
        turned[b, p] = upright
        weight = values[2 * PAR : 2 * PAR + 1]
        halves = two_parts(terms * jnp.concatenate([weight, weight], axis=1), 0)
        k = b * pairs + p
        products[:, 2 * rows * k : 2 * rows * (k + 1)] = halves

    for step in far_first[::-1]:
        records[step].wait_recv()
    for k in range(owners * pairs):
        prepare(k // pairs, k % pairs)

    swaps = []

    def scattered():
        upright = turned[...].reshape(owners * pairs * 2 * rows, LANES)
        return joined(jnp.dot(products[...], upright, preferred_element_type=jnp.float32))

    def exchange(phase, value, energy):
        mine[phase, 0:size] = value
        mine[phase, size:] = jnp.broadcast_to(energy, (WIDE, MODS))
        swap = copy(mine.at[phase], other.at[phase], swap_send.at[phase], swap_recv.at[phase], sibling)
        swap.start()
        swaps.append(swap)

    def received(phase):
        swaps[phase].wait_recv()
        both = mine[phase] + other[phase]
        return both[0:size], both[size : size + 1, 0:1]

    gradient = scattered()
    exchange(0, gradient, jnp.zeros((1, 1), jnp.float32))
    for k in range(owners * pairs):
        b, p = k // pairs, k % pairs
        hits = record[b, p, 2 * PAR + 1 : 2 * PAR + 3].astype(jnp.float32)
        named = onehot(module_ids == jnp.concatenate([hits[0:1], hits[1:2]], axis=1))
        labels[b, p, 0:MODS] = named
        labels[b, p, MODS : 2 * MODS] = named

    lane = lax.broadcasted_iota(jnp.int32, (LANES, order_size), 0)
    column = lax.broadcasted_iota(jnp.int32, (LANES, order_size), 1)
    prior = jnp.zeros((WIDE, order_size), jnp.float32)
    for j in range(pairs):
        module = lane // PAR + (2 * j + half) * (portion // PAR)
        place = onehot(
            (lane < portion) & (column == lax.rem(lane, PAR) * MODS + module)
        )
        laid = jnp.dot(three_parts(side[j]), place, preferred_element_type=jnp.float32)
        prior = prior + (laid[0:WIDE] + laid[WIDE : 2 * WIDE] + laid[2 * WIDE :])
    prior = jnp.concatenate([prior[:, i * MODS : (i + 1) * MODS] for i in range(PAR)], axis=0)

    def apply(phase, vector):
        parts = two_parts(vector, 1)
        energy = jnp.zeros((1, rows), jnp.float32)
        for k in range(owners * pairs):
            b, p = k // pairs, k % pairs
            terms = spread[b, p]
            read = jnp.dot(parts, labels[b, p], preferred_element_type=jnp.float32)
            along = jnp.sum(terms * read, axis=0, keepdims=True)
            along = along[:, 0:rows] + along[:, rows : 2 * rows]
            energy = energy + along * along
            products[:, 2 * rows * k : 2 * rows * (k + 1)] = two_parts(
                terms * jnp.concatenate([along, along], axis=1), 0
            )
        summed = scattered()
        damped = prior * vector
        exchange(phase, summed + damped, total(energy) + total(damped * vector))

    module_row = lax.broadcasted_iota(jnp.int32, (MODS, order_size), 0)
    module_of = lax.broadcasted_iota(jnp.int32, (MODS, order_size), 1) // PAR
    place = onehot(module_row == module_of)
    component = lax.broadcasted_iota(jnp.int32, (WIDE, order_size), 0)
    parameter = lax.broadcasted_iota(jnp.int32, (WIDE, order_size), 1)
    own_entry = component == lax.rem(parameter, PAR)
    own_block = lax.broadcasted_iota(jnp.int32, (WIDE, MODS), 0) == blk

    def in_order(vector):
        own = [
            jnp.sum(jnp.where(own_block, vector[i * WIDE : (i + 1) * WIDE], 0.0), axis=0, keepdims=True)
            for i in range(PAR)
        ]
        own = jnp.concatenate(own + [jnp.zeros((WIDE - PAR, MODS), jnp.float32)], axis=0)
        laid = jnp.dot(three_parts(own), place, preferred_element_type=jnp.float32)
        laid = laid[0:WIDE] + laid[WIDE : 2 * WIDE] + laid[2 * WIDE :]
        return jnp.sum(jnp.where(own_entry, laid, 0.0), axis=0, keepdims=True)

    gradient, _ = received(0)
    apply(1, gradient)
    norm = total(gradient * gradient) + epsilon
    laid_gradient = in_order(gradient)
    out_ref[1:2] = laid_gradient
    image, energy = received(1)
    first = energy / norm
    direction = image - first * gradient
    apply(2, direction)
    scale = total(direction * direction) + epsilon * norm
    below = scale / norm
    laid_direction = in_order(direction)
    image, energy = received(2)
    second = energy / scale
    rest = image - second * direction - below * gradient
    end = total(rest * rest) / scale + epsilon
    minor = first * second - below
    determinant = minor * minor + end * (first * first + below)
    out_ref[0:1] = (
        (second * minor + first * end) / determinant * laid_gradient
        - minor / determinant * laid_direction
    )
    for one in list(extras.values()) + list(records.values()) + swaps:
        one.wait_send()


def joined(summed):
    return summed[0 : PAR * WIDE, 0:MODS] + summed[PAR * WIDE :, 0:MODS]


def on_device(
    row_block,
    row_hits,
    row_slot,
    track_kept,
    row_derivs,
    row_resid,
    row_invsig,
    pattern,
    prior,
    owners,
    shares,
):
    args = (
        row_block, row_hits, row_slot, track_kept, row_derivs, row_resid, row_invsig, pattern, prior
    )
    if owners != WIDE or shares % 2 or MODS % shares:
        return on_device_large(*args)
    rows = row_resid.shape[0]
    dma = pltpu.SemaphoreType.DMA
    pairs = shares // 2
    out = pl.pallas_call(
        functools.partial(kernel, owners, shares),
        out_shape=pltpu.VMEM((2, MODS * PAR), jnp.float32),
        in_specs=[pl.BlockSpec(memory_space=pltpu.HBM)] * 9,
        out_specs=pl.BlockSpec(memory_space=pltpu.VMEM),
        scratch_shapes=[
            pltpu.VMEM((1, rows), jnp.int32),
            pltpu.VMEM((2, rows), jnp.int32),
            pltpu.VMEM((1, rows), jnp.int32),
            pltpu.VMEM((1, track_kept.shape[0]), jnp.int32),
            pltpu.VMEM((2 * PAR, rows), jnp.bfloat16),
            pltpu.VMEM((rows,), jnp.bfloat16),
            pltpu.VMEM((rows,), jnp.bfloat16),
            pltpu.VMEM((1, NB), jnp.int32),
            pltpu.VMEM((1, MODS * PAR), jnp.float32),
            dma((9,)),
            pltpu.VMEM((owners, pairs, RECORD, rows), jnp.bfloat16),
            pltpu.VMEM((owners, pairs, EXTRA, LANES), jnp.float32),
            pltpu.VMEM((owners, pairs, PAR * WIDE, 2 * rows), jnp.float32),
            pltpu.VMEM((owners, pairs, 2 * MODS, 2 * rows), jnp.bfloat16),
            pltpu.VMEM((owners, pairs, 2 * rows, LANES), jnp.bfloat16),
            pltpu.VMEM((2 * PAR * WIDE, owners * pairs * 2 * rows), jnp.bfloat16),
            pltpu.VMEM((PHASES, PAR * WIDE + WIDE, MODS), jnp.float32),
            pltpu.VMEM((PHASES, PAR * WIDE + WIDE, MODS), jnp.float32),
            dma((owners, pairs)),
            dma((owners, pairs)),
            dma((owners, pairs)),
            dma((owners, pairs)),
            dma((PHASES,)),
            dma((PHASES,)),
        ],
        compiler_params=pltpu.CompilerParams(
            collective_id=0, has_side_effects=True, vmem_limit_bytes=60 * 1024 * 1024
        ),
    )(
        row_block.reshape(1, rows),
        row_hits,
        row_slot.reshape(1, rows),
        track_kept.reshape(1, -1),
        row_derivs,
        row_resid,
        row_invsig,
        pattern,
        prior,
    )
    return out[0:1], out[1:2]


def solution(mesh):
    return jax.shard_map(
        functools.partial(on_device, owners=mesh.shape["blk"], shares=mesh.shape["trk"]),
        mesh=mesh,
        in_specs=(
            P(("blk", "trk"), None),
            P(None, ("blk", "trk")),
            P(("blk", "trk")),
            P(("blk", "trk")),
            P(None, ("blk", "trk")),
            P(("blk", "trk")),
            P(("blk", "trk")),
            P("blk", None),
            P("blk", None),
        ),
        out_specs=(P("blk", None), P("blk", None)),
        check_vma=False,
    )
```

```python
import functools

import jax
import jax.numpy as jnp
from jax import lax
from jax.experimental import pallas as pl
from jax.experimental.pallas import tpu as pltpu
from jax.sharding import PartitionSpec as P

MODS = 64
PAR = 6
NB = 5
SEG = 8
ITERS = 2


epsilon = 1e-06


def passed_along(block, axis, distance):
    devices = range(lax.axis_size(axis))
    route = [((i - distance) % len(devices), i) for i in devices]
    return lax.ppermute(block, axis, route)


def project(initial_norm, diag_terms, off_terms, basis_list):
    size_count = len(diag_terms)
    zero_value = diag_terms[0] * 0.0
    rows_list = []
    for row_index in range(size_count + 1):
        entries = []
        for column in range(size_count):
            if row_index == column:
                entries.append(diag_terms[column])
            elif row_index == column + 1:
                entries.append(off_terms[column])
            elif column == row_index + 1:
                entries.append(off_terms[row_index])
            else:
                entries.append(zero_value)
        rows_list.append(jnp.stack(entries))
    tridiagonal = jnp.stack(rows_list)
    gram_matrix = jnp.dot(tridiagonal.T, tridiagonal, precision=lax.Precision.HIGHEST)
    target = initial_norm * tridiagonal[0]
    factor = jnp.linalg.cholesky(gram_matrix)
    forward = []
    for row_index in range(size_count):
        partial_sum = target[row_index]
        for column in range(row_index):
            partial_sum = partial_sum - factor[row_index, column] * forward[column]
        forward.append(partial_sum / factor[row_index, row_index])
    backward = [zero_value] * size_count
    for row_index in reversed(range(size_count)):
        partial_sum = forward[row_index]
        for column in range(row_index + 1, size_count):
            partial_sum = partial_sum - factor[column, row_index] * backward[column]
        backward[row_index] = partial_sum / factor[row_index, row_index]
    solution = backward[0] * basis_list[0]
    row_index = 1
    solution = solution + backward[row_index] * basis_list[row_index]
    return solution


def contract(left_rows, right_rows):
    return lax.dot_general(
        left_rows, right_rows, (((0,), (0,)), ((), ())), preferred_element_type=jnp.float32
    )


def on_device_large(
    row_block, row_hits, row_slot, track_kept, row_derivs, row_resid, row_invsig, pattern, prior
):
    row_count = row_resid.shape[0]
    owners = lax.axis_size("blk")
    capacity = 2 * row_count // owners
    order_size = MODS * PAR
    kept_rows = jnp.repeat(track_kept, SEG).astype(jnp.float32)
    scaling = kept_rows * row_invsig.astype(jnp.float32)
    scaled = (scaling[None, :] * row_derivs.astype(jnp.float32)).astype(jnp.bfloat16)
    weighted = (scaling * row_resid.astype(jnp.float32)).astype(jnp.bfloat16)
    destination = row_block[:, 0]
    member = (destination[:, None] == jnp.arange(owners, dtype=jnp.int32)[None, :]).astype(
        jnp.bfloat16
    )
    row_ids = jnp.arange(row_count, dtype=jnp.int32)
    earlier = (row_ids[:, None] > row_ids[None, :]).astype(jnp.bfloat16)
    before = jnp.dot(earlier, member, preferred_element_type=jnp.float32)
    rank_within = jnp.sum(before * member.astype(jnp.float32), axis=1).astype(jnp.int32)
    slot_place = destination * capacity + rank_within
    labels = jnp.stack([row_hits[0], row_hits[1], row_slot]).astype(jnp.bfloat16)
    record = jnp.concatenate([scaled, weighted[None, :], labels], axis=0)
    outgoing = (
        jnp.zeros((record.shape[0], owners * capacity), jnp.bfloat16).at[:, slot_place].set(record)
    )
    incoming = lax.all_to_all(outgoing, "blk", split_axis=1, concat_axis=1, tiled=True)
    column_ids = jnp.arange(order_size, dtype=jnp.int32)
    column_module = column_ids // PAR
    column_param = column_ids % PAR

    def expand(values, module_ids):
        spread = jnp.zeros((values.shape[1], order_size), jnp.bfloat16)
        for component in range(PAR):
            spread = jnp.where(
                column_param[None, :] == component, values[component][:, None], spread
            )
        return jnp.where(
            module_ids[:, None] == column_module[None, :], spread, jnp.zeros_like(spread)
        )

    first_module = incoming[2 * PAR + 1].astype(jnp.int32)
    second_module = incoming[2 * PAR + 2].astype(jnp.int32)
    slot_in = incoming[2 * PAR + 3].astype(jnp.int32)
    resid_in = incoming[2 * PAR]
    first_rows = expand(incoming[0:PAR], first_module)
    second_rows = expand(incoming[PAR : 2 * PAR], second_module)
    own_block = contract(first_rows, first_rows)
    grad_own = jnp.dot(resid_in, first_rows, preferred_element_type=jnp.float32)
    cross_list, partner_list, grad_list = ([], [], [])
    for slot_id in range(NB):
        masked = jnp.where((slot_in == slot_id)[:, None], second_rows, jnp.zeros_like(second_rows))
        cross_list.append(contract(first_rows, masked))
        partner_list.append(contract(masked, masked))
        grad_list.append(jnp.dot(resid_in, masked, preferred_element_type=jnp.float32))
    cross_blocks = jnp.stack(cross_list)
    partner_blocks = jnp.stack(partner_list)
    grad_partner = jnp.stack(grad_list)
    position = lax.axis_index("blk")
    neighbours = pattern[0]
    offset = (neighbours - position) % owners
    offset = jnp.where(offset > owners // 2, offset - owners, offset)

    def deliver(own_term, partner_terms):
        local_sum = own_term + jnp.sum(
            jnp.where((offset == 0)[:, None], partner_terms, 0.0), axis=0, keepdims=True
        )
        for shift_by in (-2, -1, 1, 2):
            sending = jnp.sum(
                jnp.where((offset == shift_by)[:, None], partner_terms, 0.0), axis=0, keepdims=True
            )
            local_sum = local_sum + passed_along(sending, "blk", shift_by)
        return lax.psum(local_sum, "trk")

    gradient = deliver(grad_own[None, :], grad_partner)
    initial_norm = jnp.sqrt(lax.psum(jnp.sum(gradient * gradient), "blk") + epsilon)
    current = gradient / initial_norm
    previous = jnp.zeros_like(gradient)
    beta_term = jnp.zeros((), jnp.float32)
    diag_terms, off_terms, basis_list = ([], [], [])
    for iteration in range(ITERS):
        result = jnp.where((offset == 0)[:, None], current, 0.0)
        for fetch_shift_by in (-2, -1, 1, 2):
            arrived = passed_along(current, "blk", -fetch_shift_by)
            result = result + jnp.where((offset == fetch_shift_by)[:, None], arrived, 0.0)
        operate_own_term = jnp.dot(own_block, current[0], precision=lax.Precision.HIGHEST)
        operate_own_term = operate_own_term + jnp.einsum(
            "kij,kj->i", cross_blocks, result, precision=lax.Precision.HIGHEST
        )
        operate_partner_terms = jnp.einsum(
            "kij,i->kj", cross_blocks, current[0], precision=lax.Precision.HIGHEST
        )
        operate_partner_terms = operate_partner_terms + jnp.einsum(
            "kij,kj->ki", partner_blocks, result, precision=lax.Precision.HIGHEST
        )
        image_vec = prior * current + deliver(operate_own_term[None, :], operate_partner_terms)
        alpha_term = lax.psum(jnp.sum(current * image_vec), "blk")
        direction = image_vec - alpha_term * current - beta_term * previous
        beta_next = jnp.sqrt(lax.psum(jnp.sum(direction * direction), "blk") + epsilon)
        diag_terms.append(alpha_term)
        off_terms.append(beta_next)
        basis_list.append(current)
        previous, current, beta_term = (current, direction / beta_next, beta_next)
    solution = project(initial_norm, diag_terms, off_terms, basis_list)
    return (solution, gradient)


LANES = 128
WIDE = 8
PHASES = ITERS + 1
RECORD = 16
EXTRA = 3
MESH = pl.DeviceIdType.MESH


def three_parts(value):
    high = value.astype(jnp.bfloat16).astype(jnp.float32)
    rest = value - high
    middle = rest.astype(jnp.bfloat16).astype(jnp.float32)
    return jnp.concatenate([high, middle, rest - middle], axis=0).astype(jnp.bfloat16)


def two_parts(value, axis):
    high = value.astype(jnp.bfloat16)
    low = (value - high.astype(jnp.float32)).astype(jnp.bfloat16)
    return jnp.concatenate([high, low], axis=axis)


def total(value):
    return jnp.sum(jnp.sum(value, axis=0, keepdims=True), axis=1, keepdims=True)


def onehot(mask):
    return mask.astype(jnp.float32).astype(jnp.bfloat16)


def kernel(
    owners,
    shares,
    block_ref,
    hits_ref,
    slot_ref,
    kept_ref,
    derivs_ref,
    resid_ref,
    invsig_ref,
    pattern_ref,
    prior_ref,
    out_ref,
    block_in,
    hits_in,
    slot_in,
    kept_in,
    derivs_in,
    resid_in,
    invsig_in,
    pattern_in,
    prior_in,
    input_sem,
    record,
    extra,
    spread,
    labels,
    turned,
    products,
    mine,
    other,
    record_send,
    record_recv,
    extra_send,
    extra_recv,
    swap_send,
    swap_recv,
):
    blk, trk = lax.axis_index("blk"), lax.axis_index("trk")
    rows = block_ref.shape[1]
    tracks = kept_ref.shape[1]
    pairs = shares // 2
    pair, half = trk // 2, lax.rem(trk, 2)
    sibling = {"blk": blk, "trk": pair * 2 + 1 - half}
    order_size = MODS * PAR
    portion = order_size // shares

    me = blk * pairs + pair
    line = owners * pairs
    mirror = jnp.where(me < line // 2, 0, 1)
    place = jnp.where(mirror == 1, line - 1 - me, me)
    others = []
    for n in reversed(range(line - 1)):
        k = n + jnp.where(n >= place, 1, 0)
        others.append(jnp.where(mirror == 1, line - 1 - k, k))

    def peer(k):
        return {"blk": k // pairs, "trk": lax.rem(k, pairs) * 2 + half}

    peers = [peer(k) for k in others]
    barrier = pltpu.get_barrier_semaphore()
    for target in peers + [sibling]:
        pl.semaphore_signal(barrier, inc=1, device_id=target, device_id_type=MESH)

    outside = (
        kept_ref, invsig_ref, derivs_ref, resid_ref, block_ref, hits_ref, slot_ref, prior_ref, pattern_ref
    )
    inside = (
        kept_in, invsig_in, derivs_in, resid_in, block_in, hits_in, slot_in, prior_in, pattern_in
    )
    fetches = [
        pltpu.make_async_copy(source, target, input_sem.at[i])
        for i, (source, target) in enumerate(zip(outside, inside))
    ]
    for one in fetches:
        one.start()
    for one in fetches:
        one.wait()

    def copy(source, target, send, recv, device):
        return pltpu.make_async_remote_copy(
            src_ref=source, dst_ref=target, send_sem=send, recv_sem=recv, device_id=device, device_id_type=MESH
        )

    track_of = lax.broadcasted_iota(jnp.int32, (tracks, rows), 1) // SEG
    track_id = lax.broadcasted_iota(jnp.int32, (tracks, rows), 0)
    kept_rows = jnp.dot(
        onehot(jnp.broadcast_to(kept_in[...], (WIDE, tracks)) > 0),
        onehot(track_of == track_id),
        preferred_element_type=jnp.float32,
    )[0:1]
    scaling = kept_rows * invsig_in[...].reshape(1, rows).astype(jnp.float32)
    scaled = scaling * derivs_in[...].astype(jnp.float32)
    weighted = scaling * resid_in[...].reshape(1, rows).astype(jnp.float32)
    record[blk, pair] = jnp.concatenate(
        [scaled, weighted, hits_in[...].astype(jnp.float32), slot_in[...].astype(jnp.float32)], axis=0
    ).astype(jnp.bfloat16)
    block_row = block_in[...].astype(jnp.float32)
    for piece in range(rows // LANES):
        extra[blk, pair, piece : piece + 1] = block_row[:, piece * LANES : (piece + 1) * LANES]
    last = rows // LANES
    own = jnp.zeros((1, portion), jnp.float32)
    for t in range(shares):
        own = jnp.where(trk == t, prior_in[:, t * portion : (t + 1) * portion], own)
    extra[blk, pair, last : last + 1, 0:portion] = own
    extra[blk, pair, last : last + 1, portion : portion + NB] = pattern_in[...].astype(jnp.float32)

    pl.semaphore_wait(barrier, len(peers) + 1)
    sent, arriving = [], []
    for k, target in zip(others, peers):
        b, p = k // pairs, lax.rem(k, pairs)
        for data, send, recv in ((extra, extra_send, extra_recv), (record, record_send, record_recv)):
            sent.append(copy(data.at[blk, pair], data.at[blk, pair], send.at[b, p], recv.at[blk, pair], target))
            arriving.append(copy(data.at[b, p], data.at[b, p], send.at[b, p], recv.at[b, p], target))
    for one in sent:
        one.start()

    size = PAR * WIDE
    block_ids = lax.broadcasted_iota(jnp.int32, (WIDE, rows), 0).astype(jnp.float32)
    module_ids = lax.broadcasted_iota(jnp.int32, (MODS, 2 * rows), 0).astype(jnp.float32)
    for one in arriving:
        one.wait_recv()
    side = [extra[:, j, last, :] for j in range(pairs)]
    columns = [
        jnp.broadcast_to(side[0][:, portion + s : portion + s + 1], (WIDE, rows)) for s in range(NB)
    ]

    def prepare(b, p):
        values = record[b, p].astype(jnp.float32)
        first_block = jnp.concatenate([extra[b, p, i : i + 1] for i in range(last)], axis=1)
        first = block_ids == first_block
        slot = values[2 * PAR + 3 : 2 * PAR + 4]
        coupled = columns[0]
        for s in range(1, NB):
            coupled = jnp.where(slot == s, columns[s], coupled)
        second_block = jnp.sum(jnp.where(first, coupled, 0.0), axis=0, keepdims=True)
        second = block_ids == second_block
        terms = []
        for i in range(PAR):
            terms.append(
                jnp.concatenate(
                    [
                        jnp.where(first, values[i : i + 1], 0.0),
                        jnp.where(second, values[PAR + i : PAR + i + 1], 0.0),
                    ],
                    axis=1,
                )
            )
        terms = jnp.concatenate(terms, axis=0)
        spread[b, p] = terms
        hits = jnp.concatenate(
            [values[2 * PAR + 1 : 2 * PAR + 2], values[2 * PAR + 2 : 2 * PAR + 3]], axis=1
        )
        named = onehot(module_ids == hits)
        labels[b, p, 0:MODS] = named
        labels[b, p, MODS : 2 * MODS] = named
        upright = jnp.transpose(named)
        turned[b, p] = upright
        weight = values[2 * PAR : 2 * PAR + 1]
        halves = two_parts(terms * jnp.concatenate([weight, weight], axis=1), 0)
        k = b * pairs + p
        products[:, 2 * rows * k : 2 * rows * (k + 1)] = halves

    for k in range(owners * pairs):
        prepare(k // pairs, k % pairs)

    swaps = []

    def scattered():
        upright = turned[...].reshape(owners * pairs * 2 * rows, MODS)
        return joined(jnp.dot(products[...], upright, preferred_element_type=jnp.float32))

    def exchange(phase, value, energy):
        mine[phase, 0:size] = value
        mine[phase, size:] = jnp.broadcast_to(energy, (WIDE, MODS))
        swap = copy(mine.at[phase], other.at[phase], swap_send.at[phase], swap_recv.at[phase], sibling)
        swap.start()
        swaps.append(swap)

    def received(phase):
        swaps[phase].wait_recv()
        both = mine[phase] + other[phase]
        return both[0:size], both[size : size + 1, 0:1]

    gradient = scattered()
    exchange(0, gradient, jnp.zeros((1, 1), jnp.float32))

    lane = lax.broadcasted_iota(jnp.int32, (LANES, order_size), 0)
    column = lax.broadcasted_iota(jnp.int32, (LANES, order_size), 1)
    prior = jnp.zeros((WIDE, order_size), jnp.float32)
    for j in range(pairs):
        module = lane // PAR + (2 * j + half) * (portion // PAR)
        place = onehot(
            (lane < portion) & (column == lax.rem(lane, PAR) * MODS + module)
        )
        laid = jnp.dot(three_parts(side[j]), place, preferred_element_type=jnp.float32)
        prior = prior + (laid[0:WIDE] + laid[WIDE : 2 * WIDE] + laid[2 * WIDE :])
    prior = jnp.concatenate([prior[:, i * MODS : (i + 1) * MODS] for i in range(PAR)], axis=0)

    def apply(phase, vector):
        parts = two_parts(vector, 1)
        energy = jnp.zeros((1, rows), jnp.float32)
        for k in range(owners * pairs):
            b, p = k // pairs, k % pairs
            terms = spread[b, p]
            read = jnp.dot(parts, labels[b, p], preferred_element_type=jnp.float32)
            along = jnp.sum(terms * read, axis=0, keepdims=True)
            along = along[:, 0:rows] + along[:, rows : 2 * rows]
            energy = energy + along * along
            products[:, 2 * rows * k : 2 * rows * (k + 1)] = two_parts(
                terms * jnp.concatenate([along, along], axis=1), 0
            )
        summed = scattered()
        damped = prior * vector
        exchange(phase, summed + damped, total(energy) + total(damped * vector))

    module_row = lax.broadcasted_iota(jnp.int32, (MODS, order_size), 0)
    module_of = lax.broadcasted_iota(jnp.int32, (MODS, order_size), 1) // PAR
    place = onehot(module_row == module_of)
    component = lax.broadcasted_iota(jnp.int32, (WIDE, order_size), 0)
    parameter = lax.broadcasted_iota(jnp.int32, (WIDE, order_size), 1)
    own_entry = component == lax.rem(parameter, PAR)
    own_block = lax.broadcasted_iota(jnp.int32, (WIDE, MODS), 0) == blk

    def in_order(vector):
        own = [
            jnp.sum(jnp.where(own_block, vector[i * WIDE : (i + 1) * WIDE], 0.0), axis=0, keepdims=True)
            for i in range(PAR)
        ]
        own = jnp.concatenate(own + [jnp.zeros((WIDE - PAR, MODS), jnp.float32)], axis=0)
        laid = jnp.dot(three_parts(own), place, preferred_element_type=jnp.float32)
        laid = laid[0:WIDE] + laid[WIDE : 2 * WIDE] + laid[2 * WIDE :]
        return jnp.sum(jnp.where(own_entry, laid, 0.0), axis=0, keepdims=True)

    gradient, _ = received(0)
    apply(1, gradient)
    norm = total(gradient * gradient) + epsilon
    laid_gradient = in_order(gradient)
    out_ref[1:2] = laid_gradient
    image, energy = received(1)
    first = energy / norm
    direction = image - first * gradient
    apply(2, direction)
    scale = total(direction * direction) + epsilon * norm
    below = scale / norm
    laid_direction = in_order(direction)
    image, energy = received(2)
    second = energy / scale
    rest = image - second * direction - below * gradient
    end = total(rest * rest) / scale + epsilon
    minor = first * second - below
    determinant = minor * minor + end * (first * first + below)
    out_ref[0:1] = (
        (second * minor + first * end) / determinant * laid_gradient
        - minor / determinant * laid_direction
    )
    for one in sent + swaps:
        one.wait_send()


def joined(summed):
    return summed[0 : PAR * WIDE] + summed[PAR * WIDE :]


def on_device(
    row_block,
    row_hits,
    row_slot,
    track_kept,
    row_derivs,
    row_resid,
    row_invsig,
    pattern,
    prior,
    owners,
    shares,
):
    args = (
        row_block, row_hits, row_slot, track_kept, row_derivs, row_resid, row_invsig, pattern, prior
    )
    if owners != WIDE or shares % 2 or MODS % shares:
        return on_device_large(*args)
    rows = row_resid.shape[0]
    dma = pltpu.SemaphoreType.DMA
    pairs = shares // 2
    out = pl.pallas_call(
        functools.partial(kernel, owners, shares),
        out_shape=pltpu.VMEM((2, MODS * PAR), jnp.float32),
        in_specs=[pl.BlockSpec(memory_space=pltpu.HBM)] * 9,
        out_specs=pl.BlockSpec(memory_space=pltpu.VMEM),
        scratch_shapes=[
            pltpu.VMEM((1, rows), jnp.int32),
            pltpu.VMEM((2, rows), jnp.int32),
            pltpu.VMEM((1, rows), jnp.int32),
            pltpu.VMEM((1, track_kept.shape[0]), jnp.int32),
            pltpu.VMEM((2 * PAR, rows), jnp.bfloat16),
            pltpu.VMEM((rows,), jnp.bfloat16),
            pltpu.VMEM((rows,), jnp.bfloat16),
            pltpu.VMEM((1, NB), jnp.int32),
            pltpu.VMEM((1, MODS * PAR), jnp.float32),
            dma((9,)),
            pltpu.VMEM((owners, pairs, RECORD, rows), jnp.bfloat16),
            pltpu.VMEM((owners, pairs, EXTRA, LANES), jnp.float32),
            pltpu.VMEM((owners, pairs, PAR * WIDE, 2 * rows), jnp.float32),
            pltpu.VMEM((owners, pairs, 2 * MODS, 2 * rows), jnp.bfloat16),
            pltpu.VMEM((owners, pairs, 2 * rows, MODS), jnp.bfloat16),
            pltpu.VMEM((2 * PAR * WIDE, owners * pairs * 2 * rows), jnp.bfloat16),
            pltpu.VMEM((PHASES, PAR * WIDE + WIDE, MODS), jnp.float32),
            pltpu.VMEM((PHASES, PAR * WIDE + WIDE, MODS), jnp.float32),
            dma((owners, pairs)),
            dma((owners, pairs)),
            dma((owners, pairs)),
            dma((owners, pairs)),
            dma((PHASES,)),
            dma((PHASES,)),
        ],
        compiler_params=pltpu.CompilerParams(
            collective_id=0, has_side_effects=True, vmem_limit_bytes=60 * 1024 * 1024
        ),
    )(
        row_block.reshape(1, rows),
        row_hits,
        row_slot.reshape(1, rows),
        track_kept.reshape(1, -1),
        row_derivs,
        row_resid,
        row_invsig,
        pattern,
        prior,
    )
    return out[0:1], out[1:2]


def solution(mesh):
    return jax.shard_map(
        functools.partial(on_device, owners=mesh.shape["blk"], shares=mesh.shape["trk"]),
        mesh=mesh,
        in_specs=(
            P(("blk", "trk"), None),
            P(None, ("blk", "trk")),
            P(("blk", "trk")),
            P(("blk", "trk")),
            P(None, ("blk", "trk")),
            P(("blk", "trk")),
            P(("blk", "trk")),
            P("blk", None),
            P("blk", None),
        ),
        out_specs=(P("blk", None), P("blk", None)),
        check_vma=False,
    )
```

```python
import functools

import jax
import jax.numpy as jnp
from jax import lax
from jax.experimental import pallas as pl
from jax.experimental.pallas import tpu as pltpu
from jax.sharding import PartitionSpec as P

MODS = 64
PAR = 6
NB = 5
SEG = 8
ITERS = 2


epsilon = 1e-06


def passed_along(block, axis, distance):
    devices = range(lax.axis_size(axis))
    route = [((i - distance) % len(devices), i) for i in devices]
    return lax.ppermute(block, axis, route)


def project(initial_norm, diag_terms, off_terms, basis_list):
    size_count = len(diag_terms)
    zero_value = diag_terms[0] * 0.0
    rows_list = []
    for row_index in range(size_count + 1):
        entries = []
        for column in range(size_count):
            if row_index == column:
                entries.append(diag_terms[column])
            elif row_index == column + 1:
                entries.append(off_terms[column])
            elif column == row_index + 1:
                entries.append(off_terms[row_index])
            else:
                entries.append(zero_value)
        rows_list.append(jnp.stack(entries))
    tridiagonal = jnp.stack(rows_list)
    gram_matrix = jnp.dot(tridiagonal.T, tridiagonal, precision=lax.Precision.HIGHEST)
    target = initial_norm * tridiagonal[0]
    factor = jnp.linalg.cholesky(gram_matrix)
    forward = []
    for row_index in range(size_count):
        partial_sum = target[row_index]
        for column in range(row_index):
            partial_sum = partial_sum - factor[row_index, column] * forward[column]
        forward.append(partial_sum / factor[row_index, row_index])
    backward = [zero_value] * size_count
    for row_index in reversed(range(size_count)):
        partial_sum = forward[row_index]
        for column in range(row_index + 1, size_count):
            partial_sum = partial_sum - factor[column, row_index] * backward[column]
        backward[row_index] = partial_sum / factor[row_index, row_index]
    solution = backward[0] * basis_list[0]
    row_index = 1
    solution = solution + backward[row_index] * basis_list[row_index]
    return solution


def contract(left_rows, right_rows):
    return lax.dot_general(
        left_rows, right_rows, (((0,), (0,)), ((), ())), preferred_element_type=jnp.float32
    )


def on_device_large(
    row_block, row_hits, row_slot, track_kept, row_derivs, row_resid, row_invsig, pattern, prior
):
    row_count = row_resid.shape[0]
    owners = lax.axis_size("blk")
    capacity = 2 * row_count // owners
    order_size = MODS * PAR
    kept_rows = jnp.repeat(track_kept, SEG).astype(jnp.float32)
    scaling = kept_rows * row_invsig.astype(jnp.float32)
    scaled = (scaling[None, :] * row_derivs.astype(jnp.float32)).astype(jnp.bfloat16)
    weighted = (scaling * row_resid.astype(jnp.float32)).astype(jnp.bfloat16)
    destination = row_block[:, 0]
    member = (destination[:, None] == jnp.arange(owners, dtype=jnp.int32)[None, :]).astype(
        jnp.bfloat16
    )
    row_ids = jnp.arange(row_count, dtype=jnp.int32)
    earlier = (row_ids[:, None] > row_ids[None, :]).astype(jnp.bfloat16)
    before = jnp.dot(earlier, member, preferred_element_type=jnp.float32)
    rank_within = jnp.sum(before * member.astype(jnp.float32), axis=1).astype(jnp.int32)
    slot_place = destination * capacity + rank_within
    labels = jnp.stack([row_hits[0], row_hits[1], row_slot]).astype(jnp.bfloat16)
    record = jnp.concatenate([scaled, weighted[None, :], labels], axis=0)
    outgoing = (
        jnp.zeros((record.shape[0], owners * capacity), jnp.bfloat16).at[:, slot_place].set(record)
    )
    incoming = lax.all_to_all(outgoing, "blk", split_axis=1, concat_axis=1, tiled=True)
    column_ids = jnp.arange(order_size, dtype=jnp.int32)
    column_module = column_ids // PAR
    column_param = column_ids % PAR

    def expand(values, module_ids):
        spread = jnp.zeros((values.shape[1], order_size), jnp.bfloat16)
        for component in range(PAR):
            spread = jnp.where(
                column_param[None, :] == component, values[component][:, None], spread
            )
        return jnp.where(
            module_ids[:, None] == column_module[None, :], spread, jnp.zeros_like(spread)
        )

    first_module = incoming[2 * PAR + 1].astype(jnp.int32)
    second_module = incoming[2 * PAR + 2].astype(jnp.int32)
    slot_in = incoming[2 * PAR + 3].astype(jnp.int32)
    resid_in = incoming[2 * PAR]
    first_rows = expand(incoming[0:PAR], first_module)
    second_rows = expand(incoming[PAR : 2 * PAR], second_module)
    own_block = contract(first_rows, first_rows)
    grad_own = jnp.dot(resid_in, first_rows, preferred_element_type=jnp.float32)
    cross_list, partner_list, grad_list = ([], [], [])
    for slot_id in range(NB):
        masked = jnp.where((slot_in == slot_id)[:, None], second_rows, jnp.zeros_like(second_rows))
        cross_list.append(contract(first_rows, masked))
        partner_list.append(contract(masked, masked))
        grad_list.append(jnp.dot(resid_in, masked, preferred_element_type=jnp.float32))
    cross_blocks = jnp.stack(cross_list)
    partner_blocks = jnp.stack(partner_list)
    grad_partner = jnp.stack(grad_list)
    position = lax.axis_index("blk")
    neighbours = pattern[0]
    offset = (neighbours - position) % owners
    offset = jnp.where(offset > owners // 2, offset - owners, offset)

    def deliver(own_term, partner_terms):
        local_sum = own_term + jnp.sum(
            jnp.where((offset == 0)[:, None], partner_terms, 0.0), axis=0, keepdims=True
        )
        for shift_by in (-2, -1, 1, 2):
            sending = jnp.sum(
                jnp.where((offset == shift_by)[:, None], partner_terms, 0.0), axis=0, keepdims=True
            )
            local_sum = local_sum + passed_along(sending, "blk", shift_by)
        return lax.psum(local_sum, "trk")

    gradient = deliver(grad_own[None, :], grad_partner)
    initial_norm = jnp.sqrt(lax.psum(jnp.sum(gradient * gradient), "blk") + epsilon)
    current = gradient / initial_norm
    previous = jnp.zeros_like(gradient)
    beta_term = jnp.zeros((), jnp.float32)
    diag_terms, off_terms, basis_list = ([], [], [])
    for iteration in range(ITERS):
        result = jnp.where((offset == 0)[:, None], current, 0.0)
        for fetch_shift_by in (-2, -1, 1, 2):
            arrived = passed_along(current, "blk", -fetch_shift_by)
            result = result + jnp.where((offset == fetch_shift_by)[:, None], arrived, 0.0)
        operate_own_term = jnp.dot(own_block, current[0], precision=lax.Precision.HIGHEST)
        operate_own_term = operate_own_term + jnp.einsum(
            "kij,kj->i", cross_blocks, result, precision=lax.Precision.HIGHEST
        )
        operate_partner_terms = jnp.einsum(
            "kij,i->kj", cross_blocks, current[0], precision=lax.Precision.HIGHEST
        )
        operate_partner_terms = operate_partner_terms + jnp.einsum(
            "kij,kj->ki", partner_blocks, result, precision=lax.Precision.HIGHEST
        )
        image_vec = prior * current + deliver(operate_own_term[None, :], operate_partner_terms)
        alpha_term = lax.psum(jnp.sum(current * image_vec), "blk")
        direction = image_vec - alpha_term * current - beta_term * previous
        beta_next = jnp.sqrt(lax.psum(jnp.sum(direction * direction), "blk") + epsilon)
        diag_terms.append(alpha_term)
        off_terms.append(beta_next)
        basis_list.append(current)
        previous, current, beta_term = (current, direction / beta_next, beta_next)
    solution = project(initial_norm, diag_terms, off_terms, basis_list)
    return (solution, gradient)


LANES = 128
WIDE = 8
PHASES = ITERS + 1
RECORD = 16
EXTRA = 3
MESH = pl.DeviceIdType.MESH


def three_parts(value):
    high = value.astype(jnp.bfloat16).astype(jnp.float32)
    rest = value - high
    middle = rest.astype(jnp.bfloat16).astype(jnp.float32)
    return jnp.concatenate([high, middle, rest - middle], axis=0).astype(jnp.bfloat16)


def two_parts(value, axis):
    high = value.astype(jnp.bfloat16)
    low = (value - high.astype(jnp.float32)).astype(jnp.bfloat16)
    return jnp.concatenate([high, low], axis=axis)


def total(value):
    return jnp.sum(jnp.sum(value, axis=0, keepdims=True), axis=1, keepdims=True)


def onehot(mask):
    return mask.astype(jnp.float32).astype(jnp.bfloat16)


def kernel(
    owners,
    shares,
    block_ref,
    hits_ref,
    slot_ref,
    kept_ref,
    derivs_ref,
    resid_ref,
    invsig_ref,
    pattern_ref,
    prior_ref,
    out_ref,
    block_in,
    hits_in,
    slot_in,
    kept_in,
    derivs_in,
    resid_in,
    invsig_in,
    pattern_in,
    prior_in,
    input_sem,
    record,
    extra,
    spread,
    labels,
    turned,
    products,
    mine,
    other,
    record_send,
    record_recv,
    extra_send,
    extra_recv,
    swap_send,
    swap_recv,
):
    blk, trk = lax.axis_index("blk"), lax.axis_index("trk")
    rows = block_ref.shape[1]
    tracks = kept_ref.shape[1]
    pairs = shares // 2
    pair, half = trk // 2, lax.rem(trk, 2)
    sibling = {"blk": blk, "trk": pair * 2 + 1 - half}
    order_size = MODS * PAR
    portion = order_size // shares

    me = blk * pairs + pair
    line = owners * pairs
    mirror = jnp.where(me < line // 2, 0, 1)
    place = jnp.where(mirror == 1, line - 1 - me, me)
    others = []
    for n in reversed(range(line - 1)):
        k = n + jnp.where(n >= place, 1, 0)
        others.append(jnp.where(mirror == 1, line - 1 - k, k))

    def peer(k):
        return {"blk": k // pairs, "trk": lax.rem(k, pairs) * 2 + half}

    peers = [peer(k) for k in others]
    barrier = pltpu.get_barrier_semaphore()
    for target in peers + [sibling]:
        pl.semaphore_signal(barrier, inc=1, device_id=target, device_id_type=MESH)

    outside = (
        kept_ref, invsig_ref, derivs_ref, resid_ref, block_ref, hits_ref, slot_ref, prior_ref, pattern_ref
    )
    inside = (
        kept_in, invsig_in, derivs_in, resid_in, block_in, hits_in, slot_in, prior_in, pattern_in
    )
    fetches = [
        pltpu.make_async_copy(source, target, input_sem.at[i])
        for i, (source, target) in enumerate(zip(outside, inside))
    ]
    for one in fetches:
        one.start()
    for one in fetches:
        one.wait()

    def copy(source, target, send, recv, device):
        return pltpu.make_async_remote_copy(
            src_ref=source, dst_ref=target, send_sem=send, recv_sem=recv, device_id=device, device_id_type=MESH
        )

    track_of = lax.broadcasted_iota(jnp.int32, (tracks, rows), 1) // SEG
    track_id = lax.broadcasted_iota(jnp.int32, (tracks, rows), 0)
    kept_rows = jnp.dot(
        onehot(jnp.broadcast_to(kept_in[...], (WIDE, tracks)) > 0),
        onehot(track_of == track_id),
        preferred_element_type=jnp.float32,
    )[0:1]
    scaling = kept_rows * invsig_in[...].reshape(1, rows).astype(jnp.float32)
    scaled = scaling * derivs_in[...].astype(jnp.float32)
    weighted = scaling * resid_in[...].reshape(1, rows).astype(jnp.float32)
    record[blk, pair] = jnp.concatenate(
        [scaled, weighted, hits_in[...].astype(jnp.float32), slot_in[...].astype(jnp.float32)], axis=0
    ).astype(jnp.bfloat16)
    block_row = block_in[...].astype(jnp.float32)
    for piece in range(rows // LANES):
        extra[blk, pair, piece : piece + 1] = block_row[:, piece * LANES : (piece + 1) * LANES]
    last = rows // LANES
    own = jnp.zeros((1, portion), jnp.float32)
    for t in range(shares):
        own = jnp.where(trk == t, prior_in[:, t * portion : (t + 1) * portion], own)
    extra[blk, pair, last : last + 1, 0:portion] = own
    extra[blk, pair, last : last + 1, portion : portion + NB] = pattern_in[...].astype(jnp.float32)

    pl.semaphore_wait(barrier, len(peers) + 1)
    sent, arriving = [], []
    for k, target in zip(others, peers):
        b, p = k // pairs, lax.rem(k, pairs)
        for data, send, recv in ((extra, extra_send, extra_recv), (record, record_send, record_recv)):
            sent.append(copy(data.at[blk, pair], data.at[blk, pair], send.at[b, p], recv.at[blk, pair], target))
            arriving.append(copy(data.at[b, p], data.at[b, p], send.at[b, p], recv.at[b, p], target))
    for one in sent:
        one.start()

    size = PAR * WIDE
    block_ids = lax.broadcasted_iota(jnp.int32, (WIDE, rows), 0).astype(jnp.float32)
    module_ids = lax.broadcasted_iota(jnp.int32, (MODS, 2 * rows), 0).astype(jnp.float32).astype(jnp.bfloat16)
    unit = jnp.ones((MODS, 2 * rows), jnp.bfloat16)
    for one in arriving:
        one.wait_recv()
    side = [extra[:, j, last, :] for j in range(pairs)]
    columns = [
        jnp.broadcast_to(side[0][:, portion + s : portion + s + 1], (WIDE, rows)) for s in range(NB)
    ]

    def prepare(b, p):
        values = record[b, p].astype(jnp.float32)
        first_block = jnp.concatenate([extra[b, p, i : i + 1] for i in range(last)], axis=1)
        first = block_ids == first_block
        slot = values[2 * PAR + 3 : 2 * PAR + 4]
        coupled = columns[0]
        for s in range(1, NB):
            coupled = jnp.where(slot == s, columns[s], coupled)
        second_block = jnp.sum(jnp.where(first, coupled, 0.0), axis=0, keepdims=True)
        second = block_ids == second_block
        terms = []
        for i in range(PAR):
            terms.append(
                jnp.concatenate(
                    [
                        jnp.where(first, values[i : i + 1], 0.0),
                        jnp.where(second, values[PAR + i : PAR + i + 1], 0.0),
                    ],
                    axis=1,
                )
            )
        terms = jnp.concatenate(terms, axis=0)
        spread[b, p] = terms
        labels_in = record[b, p, 2 * PAR : 2 * PAR + 3]
        weight = jnp.concatenate([labels_in[0:1], labels_in[0:1]], axis=1)
        hits = jnp.concatenate([labels_in[1:2], labels_in[2:3]], axis=1)
        match = module_ids == hits
        named = jnp.where(match, unit, jnp.zeros_like(unit))
        heavy = jnp.where(match, jnp.broadcast_to(weight, match.shape), jnp.zeros_like(unit))
        labels[b, p, 0:MODS] = named
        labels[b, p, MODS : 2 * MODS] = named
        turned[b, p] = jnp.transpose(jnp.concatenate([named, heavy], axis=0))
        k = b * pairs + p
        products[0:size, 2 * rows * k : 2 * rows * (k + 1)] = terms.astype(jnp.bfloat16)

    for k in range(owners * pairs):
        prepare(k // pairs, k % pairs)

    swaps = []

    def scattered(count):
        upright = turned[...].reshape(owners * pairs * 2 * rows, LANES)
        return jnp.dot(products[0:count], upright, preferred_element_type=jnp.float32)

    def exchange(phase, value, energy):
        mine[phase, 0:size] = value
        mine[phase, size:] = jnp.broadcast_to(energy, (WIDE, MODS))
        swap = copy(mine.at[phase], other.at[phase], swap_send.at[phase], swap_recv.at[phase], sibling)
        swap.start()
        swaps.append(swap)

    def received(phase):
        swaps[phase].wait_recv()
        both = mine[phase] + other[phase]
        return both[0:size], both[size : size + 1, 0:1]

    gradient = scattered(size)[:, MODS:]
    exchange(0, gradient, jnp.zeros((1, 1), jnp.float32))

    lane = lax.broadcasted_iota(jnp.int32, (LANES, order_size), 0)
    column = lax.broadcasted_iota(jnp.int32, (LANES, order_size), 1)
    prior = jnp.zeros((WIDE, order_size), jnp.float32)
    for j in range(pairs):
        module = lane // PAR + (2 * j + half) * (portion // PAR)
        place = onehot(
            (lane < portion) & (column == lax.rem(lane, PAR) * MODS + module)
        )
        laid = jnp.dot(three_parts(side[j]), place, preferred_element_type=jnp.float32)
        prior = prior + (laid[0:WIDE] + laid[WIDE : 2 * WIDE] + laid[2 * WIDE :])
    prior = jnp.concatenate([prior[:, i * MODS : (i + 1) * MODS] for i in range(PAR)], axis=0)

    def apply(phase, vector):
        parts = two_parts(vector, 1)
        energy = jnp.zeros((1, rows), jnp.float32)
        for k in range(owners * pairs):
            b, p = k // pairs, k % pairs
            terms = spread[b, p]
            read = jnp.dot(parts, labels[b, p], preferred_element_type=jnp.float32)
            along = jnp.sum(terms * read, axis=0, keepdims=True)
            along = along[:, 0:rows] + along[:, rows : 2 * rows]
            energy = energy + along * along
            products[:, 2 * rows * k : 2 * rows * (k + 1)] = two_parts(
                terms * jnp.concatenate([along, along], axis=1), 0
            )
        summed = scattered(2 * size)
        summed = summed[0:size, 0:MODS] + summed[size:, 0:MODS]
        damped = prior * vector
        exchange(phase, summed + damped, total(energy) + total(damped * vector))

    module_row = lax.broadcasted_iota(jnp.int32, (MODS, order_size), 0)
    module_of = lax.broadcasted_iota(jnp.int32, (MODS, order_size), 1) // PAR
    place = onehot(module_row == module_of)
    component = lax.broadcasted_iota(jnp.int32, (WIDE, order_size), 0)
    parameter = lax.broadcasted_iota(jnp.int32, (WIDE, order_size), 1)
    own_entry = component == lax.rem(parameter, PAR)
    own_block = lax.broadcasted_iota(jnp.int32, (WIDE, MODS), 0) == blk

    def in_order(vector):
        own = [
            jnp.sum(jnp.where(own_block, vector[i * WIDE : (i + 1) * WIDE], 0.0), axis=0, keepdims=True)
            for i in range(PAR)
        ]
        own = jnp.concatenate(own + [jnp.zeros((WIDE - PAR, MODS), jnp.float32)], axis=0)
        laid = jnp.dot(three_parts(own), place, preferred_element_type=jnp.float32)
        laid = laid[0:WIDE] + laid[WIDE : 2 * WIDE] + laid[2 * WIDE :]
        return jnp.sum(jnp.where(own_entry, laid, 0.0), axis=0, keepdims=True)

    gradient, _ = received(0)
    apply(1, gradient)
    norm = total(gradient * gradient) + epsilon
    laid_gradient = in_order(gradient)
    out_ref[1:2] = laid_gradient
    image, energy = received(1)
    first = energy / norm
    direction = image - first * gradient
    apply(2, direction)
    scale = total(direction * direction) + epsilon * norm
    below = scale / norm
    laid_direction = in_order(direction)
    image, energy = received(2)
    second = energy / scale
    rest = image - second * direction - below * gradient
    end = total(rest * rest) / scale + epsilon
    minor = first * second - below
    determinant = minor * minor + end * (first * first + below)
    out_ref[0:1] = (
        (second * minor + first * end) / determinant * laid_gradient
        - minor / determinant * laid_direction
    )
    for one in sent + swaps:
        one.wait_send()


def on_device(
    row_block,
    row_hits,
    row_slot,
    track_kept,
    row_derivs,
    row_resid,
    row_invsig,
    pattern,
    prior,
    owners,
    shares,
):
    args = (
        row_block, row_hits, row_slot, track_kept, row_derivs, row_resid, row_invsig, pattern, prior
    )
    if owners != WIDE or 2 * MODS != LANES or shares % 2 or MODS % shares:
        return on_device_large(*args)
    rows = row_resid.shape[0]
    dma = pltpu.SemaphoreType.DMA
    pairs = shares // 2
    out = pl.pallas_call(
        functools.partial(kernel, owners, shares),
        out_shape=pltpu.VMEM((2, MODS * PAR), jnp.float32),
        in_specs=[pl.BlockSpec(memory_space=pltpu.HBM)] * 9,
        out_specs=pl.BlockSpec(memory_space=pltpu.VMEM),
        scratch_shapes=[
            pltpu.VMEM((1, rows), jnp.int32),
            pltpu.VMEM((2, rows), jnp.int32),
            pltpu.VMEM((1, rows), jnp.int32),
            pltpu.VMEM((1, track_kept.shape[0]), jnp.int32),
            pltpu.VMEM((2 * PAR, rows), jnp.bfloat16),
            pltpu.VMEM((rows,), jnp.bfloat16),
            pltpu.VMEM((rows,), jnp.bfloat16),
            pltpu.VMEM((1, NB), jnp.int32),
            pltpu.VMEM((1, MODS * PAR), jnp.float32),
            dma((9,)),
            pltpu.VMEM((owners, pairs, RECORD, rows), jnp.bfloat16),
            pltpu.VMEM((owners, pairs, EXTRA, LANES), jnp.float32),
            pltpu.VMEM((owners, pairs, PAR * WIDE, 2 * rows), jnp.float32),
            pltpu.VMEM((owners, pairs, 2 * MODS, 2 * rows), jnp.bfloat16),
            pltpu.VMEM((owners, pairs, 2 * rows, LANES), jnp.bfloat16),
            pltpu.VMEM((2 * PAR * WIDE, owners * pairs * 2 * rows), jnp.bfloat16),
            pltpu.VMEM((PHASES, PAR * WIDE + WIDE, MODS), jnp.float32),
            pltpu.VMEM((PHASES, PAR * WIDE + WIDE, MODS), jnp.float32),
            dma((owners, pairs)),
            dma((owners, pairs)),
            dma((owners, pairs)),
            dma((owners, pairs)),
            dma((PHASES,)),
            dma((PHASES,)),
        ],
        compiler_params=pltpu.CompilerParams(
            collective_id=0, has_side_effects=True, vmem_limit_bytes=60 * 1024 * 1024
        ),
    )(
        row_block.reshape(1, rows),
        row_hits,
        row_slot.reshape(1, rows),
        track_kept.reshape(1, -1),
        row_derivs,
        row_resid,
        row_invsig,
        pattern,
        prior,
    )
    return out[0:1], out[1:2]


def solution(mesh):
    return jax.shard_map(
        functools.partial(on_device, owners=mesh.shape["blk"], shares=mesh.shape["trk"]),
        mesh=mesh,
        in_specs=(
            P(("blk", "trk"), None),
            P(None, ("blk", "trk")),
            P(("blk", "trk")),
            P(("blk", "trk")),
            P(None, ("blk", "trk")),
            P(("blk", "trk")),
            P(("blk", "trk")),
            P("blk", None),
            P("blk", None),
        ),
        out_specs=(P("blk", None), P("blk", None)),
        check_vma=False,
    )
```

```python
import functools

import jax
import jax.numpy as jnp
from jax import lax
from jax.experimental import pallas as pl
from jax.experimental.pallas import tpu as pltpu
from jax.sharding import PartitionSpec as P

MODS = 64
PAR = 6
NB = 5
SEG = 8
ITERS = 2


epsilon = 1e-06


def passed_along(block, axis, distance):
    devices = range(lax.axis_size(axis))
    route = [((i - distance) % len(devices), i) for i in devices]
    return lax.ppermute(block, axis, route)


def project(initial_norm, diag_terms, off_terms, basis_list):
    size_count = len(diag_terms)
    zero_value = diag_terms[0] * 0.0
    rows_list = []
    for row_index in range(size_count + 1):
        entries = []
        for column in range(size_count):
            if row_index == column:
                entries.append(diag_terms[column])
            elif row_index == column + 1:
                entries.append(off_terms[column])
            elif column == row_index + 1:
                entries.append(off_terms[row_index])
            else:
                entries.append(zero_value)
        rows_list.append(jnp.stack(entries))
    tridiagonal = jnp.stack(rows_list)
    gram_matrix = jnp.dot(tridiagonal.T, tridiagonal, precision=lax.Precision.HIGHEST)
    target = initial_norm * tridiagonal[0]
    factor = jnp.linalg.cholesky(gram_matrix)
    forward = []
    for row_index in range(size_count):
        partial_sum = target[row_index]
        for column in range(row_index):
            partial_sum = partial_sum - factor[row_index, column] * forward[column]
        forward.append(partial_sum / factor[row_index, row_index])
    backward = [zero_value] * size_count
    for row_index in reversed(range(size_count)):
        partial_sum = forward[row_index]
        for column in range(row_index + 1, size_count):
            partial_sum = partial_sum - factor[column, row_index] * backward[column]
        backward[row_index] = partial_sum / factor[row_index, row_index]
    solution = backward[0] * basis_list[0]
    row_index = 1
    solution = solution + backward[row_index] * basis_list[row_index]
    return solution


def contract(left_rows, right_rows):
    return lax.dot_general(
        left_rows, right_rows, (((0,), (0,)), ((), ())), preferred_element_type=jnp.float32
    )


def on_device_large(
    row_block, row_hits, row_slot, track_kept, row_derivs, row_resid, row_invsig, pattern, prior
):
    row_count = row_resid.shape[0]
    owners = lax.axis_size("blk")
    capacity = 2 * row_count // owners
    order_size = MODS * PAR
    kept_rows = jnp.repeat(track_kept, SEG).astype(jnp.float32)
    scaling = kept_rows * row_invsig.astype(jnp.float32)
    scaled = (scaling[None, :] * row_derivs.astype(jnp.float32)).astype(jnp.bfloat16)
    weighted = (scaling * row_resid.astype(jnp.float32)).astype(jnp.bfloat16)
    destination = row_block[:, 0]
    member = (destination[:, None] == jnp.arange(owners, dtype=jnp.int32)[None, :]).astype(
        jnp.bfloat16
    )
    row_ids = jnp.arange(row_count, dtype=jnp.int32)
    earlier = (row_ids[:, None] > row_ids[None, :]).astype(jnp.bfloat16)
    before = jnp.dot(earlier, member, preferred_element_type=jnp.float32)
    rank_within = jnp.sum(before * member.astype(jnp.float32), axis=1).astype(jnp.int32)
    slot_place = destination * capacity + rank_within
    labels = jnp.stack([row_hits[0], row_hits[1], row_slot]).astype(jnp.bfloat16)
    record = jnp.concatenate([scaled, weighted[None, :], labels], axis=0)
    outgoing = (
        jnp.zeros((record.shape[0], owners * capacity), jnp.bfloat16).at[:, slot_place].set(record)
    )
    incoming = lax.all_to_all(outgoing, "blk", split_axis=1, concat_axis=1, tiled=True)
    column_ids = jnp.arange(order_size, dtype=jnp.int32)
    column_module = column_ids // PAR
    column_param = column_ids % PAR

    def expand(values, module_ids):
        spread = jnp.zeros((values.shape[1], order_size), jnp.bfloat16)
        for component in range(PAR):
            spread = jnp.where(
                column_param[None, :] == component, values[component][:, None], spread
            )
        return jnp.where(
            module_ids[:, None] == column_module[None, :], spread, jnp.zeros_like(spread)
        )

    first_module = incoming[2 * PAR + 1].astype(jnp.int32)
    second_module = incoming[2 * PAR + 2].astype(jnp.int32)
    slot_in = incoming[2 * PAR + 3].astype(jnp.int32)
    resid_in = incoming[2 * PAR]
    first_rows = expand(incoming[0:PAR], first_module)
    second_rows = expand(incoming[PAR : 2 * PAR], second_module)
    own_block = contract(first_rows, first_rows)
    grad_own = jnp.dot(resid_in, first_rows, preferred_element_type=jnp.float32)
    cross_list, partner_list, grad_list = ([], [], [])
    for slot_id in range(NB):
        masked = jnp.where((slot_in == slot_id)[:, None], second_rows, jnp.zeros_like(second_rows))
        cross_list.append(contract(first_rows, masked))
        partner_list.append(contract(masked, masked))
        grad_list.append(jnp.dot(resid_in, masked, preferred_element_type=jnp.float32))
    cross_blocks = jnp.stack(cross_list)
    partner_blocks = jnp.stack(partner_list)
    grad_partner = jnp.stack(grad_list)
    position = lax.axis_index("blk")
    neighbours = pattern[0]
    offset = (neighbours - position) % owners
    offset = jnp.where(offset > owners // 2, offset - owners, offset)

    def deliver(own_term, partner_terms):
        local_sum = own_term + jnp.sum(
            jnp.where((offset == 0)[:, None], partner_terms, 0.0), axis=0, keepdims=True
        )
        for shift_by in (-2, -1, 1, 2):
            sending = jnp.sum(
                jnp.where((offset == shift_by)[:, None], partner_terms, 0.0), axis=0, keepdims=True
            )
            local_sum = local_sum + passed_along(sending, "blk", shift_by)
        return lax.psum(local_sum, "trk")

    gradient = deliver(grad_own[None, :], grad_partner)
    initial_norm = jnp.sqrt(lax.psum(jnp.sum(gradient * gradient), "blk") + epsilon)
    current = gradient / initial_norm
    previous = jnp.zeros_like(gradient)
    beta_term = jnp.zeros((), jnp.float32)
    diag_terms, off_terms, basis_list = ([], [], [])
    for iteration in range(ITERS):
        result = jnp.where((offset == 0)[:, None], current, 0.0)
        for fetch_shift_by in (-2, -1, 1, 2):
            arrived = passed_along(current, "blk", -fetch_shift_by)
            result = result + jnp.where((offset == fetch_shift_by)[:, None], arrived, 0.0)
        operate_own_term = jnp.dot(own_block, current[0], precision=lax.Precision.HIGHEST)
        operate_own_term = operate_own_term + jnp.einsum(
            "kij,kj->i", cross_blocks, result, precision=lax.Precision.HIGHEST
        )
        operate_partner_terms = jnp.einsum(
            "kij,i->kj", cross_blocks, current[0], precision=lax.Precision.HIGHEST
        )
        operate_partner_terms = operate_partner_terms + jnp.einsum(
            "kij,kj->ki", partner_blocks, result, precision=lax.Precision.HIGHEST
        )
        image_vec = prior * current + deliver(operate_own_term[None, :], operate_partner_terms)
        alpha_term = lax.psum(jnp.sum(current * image_vec), "blk")
        direction = image_vec - alpha_term * current - beta_term * previous
        beta_next = jnp.sqrt(lax.psum(jnp.sum(direction * direction), "blk") + epsilon)
        diag_terms.append(alpha_term)
        off_terms.append(beta_next)
        basis_list.append(current)
        previous, current, beta_term = (current, direction / beta_next, beta_next)
    solution = project(initial_norm, diag_terms, off_terms, basis_list)
    return (solution, gradient)


LANES = 128
WIDE = 8
PHASES = ITERS + 1
RECORD = 16
EXTRA = 3
MESH = pl.DeviceIdType.MESH


def three_parts(value):
    high = value.astype(jnp.bfloat16).astype(jnp.float32)
    rest = value - high
    middle = rest.astype(jnp.bfloat16).astype(jnp.float32)
    return jnp.concatenate([high, middle, rest - middle], axis=0).astype(jnp.bfloat16)


def two_parts(value, axis):
    high = value.astype(jnp.bfloat16)
    low = (value - high.astype(jnp.float32)).astype(jnp.bfloat16)
    return jnp.concatenate([high, low], axis=axis)


def total(value):
    return jnp.sum(jnp.sum(value, axis=0, keepdims=True), axis=1, keepdims=True)


def onehot(mask):
    return mask.astype(jnp.float32).astype(jnp.bfloat16)


def kernel(
    owners,
    shares,
    block_ref,
    hits_ref,
    slot_ref,
    kept_ref,
    derivs_ref,
    resid_ref,
    invsig_ref,
    pattern_ref,
    prior_ref,
    out_ref,
    block_in,
    hits_in,
    slot_in,
    kept_in,
    derivs_in,
    resid_in,
    invsig_in,
    pattern_in,
    prior_in,
    input_sem,
    record,
    extra,
    spread,
    labels,
    turned,
    products,
    mine,
    other,
    record_send,
    record_recv,
    extra_send,
    extra_recv,
    swap_send,
    swap_recv,
):
    blk, trk = lax.axis_index("blk"), lax.axis_index("trk")
    rows = block_ref.shape[1]
    tracks = kept_ref.shape[1]
    pairs = shares // 2
    pair, half = trk // 2, lax.rem(trk, 2)
    sibling = {"blk": blk, "trk": pair * 2 + 1 - half}
    order_size = MODS * PAR
    portion = order_size // shares

    me = blk * pairs + pair
    line = owners * pairs
    mirror = jnp.where(me < line // 2, 0, 1)
    place = jnp.where(mirror == 1, line - 1 - me, me)
    others = []
    for n in reversed(range(line - 1)):
        k = n + jnp.where(n >= place, 1, 0)
        others.append(jnp.where(mirror == 1, line - 1 - k, k))

    def peer(k):
        return {"blk": k // pairs, "trk": lax.rem(k, pairs) * 2 + half}

    peers = [peer(k) for k in others]
    barrier = pltpu.get_barrier_semaphore()
    for target in peers + [sibling]:
        pl.semaphore_signal(barrier, inc=1, device_id=target, device_id_type=MESH)

    outside = (
        kept_ref, invsig_ref, derivs_ref, resid_ref, block_ref, hits_ref, slot_ref, prior_ref, pattern_ref
    )
    inside = (
        kept_in, invsig_in, derivs_in, resid_in, block_in, hits_in, slot_in, prior_in, pattern_in
    )
    fetches = [
        pltpu.make_async_copy(source, target, input_sem.at[i])
        for i, (source, target) in enumerate(zip(outside, inside))
    ]
    for one in fetches:
        one.start()
    for one in fetches:
        one.wait()

    def copy(source, target, send, recv, device):
        return pltpu.make_async_remote_copy(
            src_ref=source, dst_ref=target, send_sem=send, recv_sem=recv, device_id=device, device_id_type=MESH
        )

    track_of = lax.broadcasted_iota(jnp.int32, (tracks, rows), 1) // SEG
    track_id = lax.broadcasted_iota(jnp.int32, (tracks, rows), 0)
    kept_rows = jnp.dot(
        onehot(jnp.broadcast_to(kept_in[...], (WIDE, tracks)) > 0),
        onehot(track_of == track_id),
        preferred_element_type=jnp.float32,
    )[0:1]
    scaling = kept_rows * invsig_in[...].reshape(1, rows).astype(jnp.float32)
    scaled = scaling * derivs_in[...].astype(jnp.float32)
    weighted = scaling * resid_in[...].reshape(1, rows).astype(jnp.float32)
    record[me] = jnp.concatenate(
        [scaled, weighted, hits_in[...].astype(jnp.float32), slot_in[...].astype(jnp.float32)], axis=0
    ).astype(jnp.bfloat16)
    block_row = block_in[...].astype(jnp.float32)
    for piece in range(rows // LANES):
        extra[me, piece : piece + 1] = block_row[:, piece * LANES : (piece + 1) * LANES]
    last = rows // LANES
    own = jnp.zeros((1, portion), jnp.float32)
    for t in range(shares):
        own = jnp.where(trk == t, prior_in[:, t * portion : (t + 1) * portion], own)
    extra[me, last : last + 1, 0:portion] = own
    extra[me, last : last + 1, portion : portion + NB] = pattern_in[...].astype(jnp.float32)

    pl.semaphore_wait(barrier, len(peers) + 1)
    sent = []
    for k, target in zip(others, peers):
        b, p = k // pairs, lax.rem(k, pairs)
        for data, send, recv in ((extra, extra_send, extra_recv), (record, record_send, record_recv)):
            sent.append(copy(data.at[me], data.at[me], send.at[b, p], recv.at[0], target))
    for one in sent:
        one.start()

    size = PAR * WIDE
    block_ids = lax.broadcasted_iota(jnp.int32, (WIDE, rows), 0).astype(jnp.float32)
    module_ids = lax.broadcasted_iota(jnp.int32, (MODS, 2 * rows), 0).astype(jnp.float32).astype(jnp.bfloat16)
    unit = jnp.ones((MODS, 2 * rows), jnp.bfloat16)
    rest_of = pl.ds(0, len(peers))
    for data, send, recv in ((extra, extra_send, extra_recv), (record, record_send, record_recv)):
        copy(data.at[rest_of], data.at[rest_of], send.at[0, 0], recv.at[0], sibling).wait_recv()
    side = [
        jnp.concatenate([extra[b * pairs + j, last : last + 1] for b in range(owners)], axis=0) for j in range(pairs)
    ]
    columns = [
        jnp.broadcast_to(side[0][:, portion + s : portion + s + 1], (WIDE, rows)) for s in range(NB)
    ]

    def prepare(b, p):
        values = record[b * pairs + p].astype(jnp.float32)
        first_block = jnp.concatenate([extra[b * pairs + p, i : i + 1] for i in range(last)], axis=1)
        first = block_ids == first_block
        slot = values[2 * PAR + 3 : 2 * PAR + 4]
        coupled = columns[0]
        for s in range(1, NB):
            coupled = jnp.where(slot == s, columns[s], coupled)
        second_block = jnp.sum(jnp.where(first, coupled, 0.0), axis=0, keepdims=True)
        second = block_ids == second_block
        terms = []
        for i in range(PAR):
            terms.append(
                jnp.concatenate(
                    [
                        jnp.where(first, values[i : i + 1], 0.0),
                        jnp.where(second, values[PAR + i : PAR + i + 1], 0.0),
                    ],
                    axis=1,
                )
            )
        terms = jnp.concatenate(terms, axis=0)
        spread[b, p] = terms
        labels_in = record[b * pairs + p, 2 * PAR : 2 * PAR + 3]
        weight = jnp.concatenate([labels_in[0:1], labels_in[0:1]], axis=1)
        hits = jnp.concatenate([labels_in[1:2], labels_in[2:3]], axis=1)
        match = module_ids == hits
        named = jnp.where(match, unit, jnp.zeros_like(unit))
        heavy = jnp.where(match, jnp.broadcast_to(weight, match.shape), jnp.zeros_like(unit))
        labels[b, p, 0:MODS] = named
        labels[b, p, MODS : 2 * MODS] = named
        turned[b, p] = jnp.transpose(jnp.concatenate([named, heavy], axis=0))
        k = b * pairs + p
        products[0:size, 2 * rows * k : 2 * rows * (k + 1)] = terms.astype(jnp.bfloat16)

    for k in range(owners * pairs):
        prepare(k // pairs, k % pairs)

    swaps = []

    def scattered(count):
        upright = turned[...].reshape(owners * pairs * 2 * rows, LANES)
        return jnp.dot(products[0:count], upright, preferred_element_type=jnp.float32)

    def exchange(phase, value, energy):
        mine[phase, 0:size] = value
        mine[phase, size:] = jnp.broadcast_to(energy, (WIDE, MODS))
        swap = copy(mine.at[phase], other.at[phase], swap_send.at[phase], swap_recv.at[phase], sibling)
        swap.start()
        swaps.append(swap)

    def received(phase):
        swaps[phase].wait_recv()
        both = mine[phase] + other[phase]
        return both[0:size], both[size : size + 1, 0:1]

    gradient = scattered(size)[:, MODS:]
    exchange(0, gradient, jnp.zeros((1, 1), jnp.float32))

    lane = lax.broadcasted_iota(jnp.int32, (LANES, order_size), 0)
    column = lax.broadcasted_iota(jnp.int32, (LANES, order_size), 1)
    prior = jnp.zeros((WIDE, order_size), jnp.float32)
    for j in range(pairs):
        module = lane // PAR + (2 * j + half) * (portion // PAR)
        place = onehot(
            (lane < portion) & (column == lax.rem(lane, PAR) * MODS + module)
        )
        laid = jnp.dot(three_parts(side[j]), place, preferred_element_type=jnp.float32)
        prior = prior + (laid[0:WIDE] + laid[WIDE : 2 * WIDE] + laid[2 * WIDE :])
    prior = jnp.concatenate([prior[:, i * MODS : (i + 1) * MODS] for i in range(PAR)], axis=0)

    def apply(phase, vector):
        parts = two_parts(vector, 1)
        energy = jnp.zeros((1, rows), jnp.float32)
        for k in range(owners * pairs):
            b, p = k // pairs, k % pairs
            terms = spread[b, p]
            read = jnp.dot(parts, labels[b, p], preferred_element_type=jnp.float32)
            along = jnp.sum(terms * read, axis=0, keepdims=True)
            along = along[:, 0:rows] + along[:, rows : 2 * rows]
            energy = energy + along * along
            products[:, 2 * rows * k : 2 * rows * (k + 1)] = two_parts(
                terms * jnp.concatenate([along, along], axis=1), 0
            )
        summed = scattered(2 * size)
        summed = summed[0:size, 0:MODS] + summed[size:, 0:MODS]
        damped = prior * vector
        exchange(phase, summed + damped, total(energy) + total(damped * vector))

    module_row = lax.broadcasted_iota(jnp.int32, (MODS, order_size), 0)
    module_of = lax.broadcasted_iota(jnp.int32, (MODS, order_size), 1) // PAR
    place = onehot(module_row == module_of)
    component = lax.broadcasted_iota(jnp.int32, (WIDE, order_size), 0)
    parameter = lax.broadcasted_iota(jnp.int32, (WIDE, order_size), 1)
    own_entry = component == lax.rem(parameter, PAR)
    own_block = lax.broadcasted_iota(jnp.int32, (WIDE, MODS), 0) == blk

    def in_order(vector):
        own = [
            jnp.sum(jnp.where(own_block, vector[i * WIDE : (i + 1) * WIDE], 0.0), axis=0, keepdims=True)
            for i in range(PAR)
        ]
        own = jnp.concatenate(own + [jnp.zeros((WIDE - PAR, MODS), jnp.float32)], axis=0)
        laid = jnp.dot(three_parts(own), place, preferred_element_type=jnp.float32)
        laid = laid[0:WIDE] + laid[WIDE : 2 * WIDE] + laid[2 * WIDE :]
        return jnp.sum(jnp.where(own_entry, laid, 0.0), axis=0, keepdims=True)

    for one in sent:
        one.wait_send()
    gradient, _ = received(0)
    apply(1, gradient)
    norm = total(gradient * gradient) + epsilon
    laid_gradient = in_order(gradient)
    out_ref[1:2] = laid_gradient
    swaps[0].wait_send()
    image, energy = received(1)
    first = energy / norm
    direction = image - first * gradient
    apply(2, direction)
    scale = total(direction * direction) + epsilon * norm
    below = scale / norm
    laid_direction = in_order(direction)
    swaps[1].wait_send()
    image, energy = received(2)
    second = energy / scale
    rest = image - second * direction - below * gradient
    end = total(rest * rest) / scale + epsilon
    minor = first * second - below
    determinant = minor * minor + end * (first * first + below)
    out_ref[0:1] = (
        (second * minor + first * end) / determinant * laid_gradient
        - minor / determinant * laid_direction
    )
    swaps[-1].wait_send()


def on_device(
    row_block,
    row_hits,
    row_slot,
    track_kept,
    row_derivs,
    row_resid,
    row_invsig,
    pattern,
    prior,
    owners,
    shares,
):
    args = (
        row_block, row_hits, row_slot, track_kept, row_derivs, row_resid, row_invsig, pattern, prior
    )
    if owners != WIDE or 2 * MODS != LANES or shares % 2 or MODS % shares:
        return on_device_large(*args)
    rows = row_resid.shape[0]
    dma = pltpu.SemaphoreType.DMA
    pairs = shares // 2
    out = pl.pallas_call(
        functools.partial(kernel, owners, shares),
        out_shape=pltpu.VMEM((2, MODS * PAR), jnp.float32),
        in_specs=[pl.BlockSpec(memory_space=pltpu.HBM)] * 9,
        out_specs=pl.BlockSpec(memory_space=pltpu.VMEM),
        scratch_shapes=[
            pltpu.VMEM((1, rows), jnp.int32),
            pltpu.VMEM((2, rows), jnp.int32),
            pltpu.VMEM((1, rows), jnp.int32),
            pltpu.VMEM((1, track_kept.shape[0]), jnp.int32),
            pltpu.VMEM((2 * PAR, rows), jnp.bfloat16),
            pltpu.VMEM((rows,), jnp.bfloat16),
            pltpu.VMEM((rows,), jnp.bfloat16),
            pltpu.VMEM((1, NB), jnp.int32),
            pltpu.VMEM((1, MODS * PAR), jnp.float32),
            dma((9,)),
            pltpu.VMEM((owners * pairs, RECORD, rows), jnp.bfloat16),
            pltpu.VMEM((owners * pairs, EXTRA, LANES), jnp.float32),
            pltpu.VMEM((owners, pairs, PAR * WIDE, 2 * rows), jnp.float32),
            pltpu.VMEM((owners, pairs, 2 * MODS, 2 * rows), jnp.bfloat16),
            pltpu.VMEM((owners, pairs, 2 * rows, LANES), jnp.bfloat16),
            pltpu.VMEM((2 * PAR * WIDE, owners * pairs * 2 * rows), jnp.bfloat16),
            pltpu.VMEM((PHASES, PAR * WIDE + WIDE, MODS), jnp.float32),
            pltpu.VMEM((PHASES, PAR * WIDE + WIDE, MODS), jnp.float32),
            dma((owners, pairs)),
            dma((1,)),
            dma((owners, pairs)),
            dma((1,)),
            dma((PHASES,)),
            dma((PHASES,)),
        ],
        compiler_params=pltpu.CompilerParams(
            collective_id=0, has_side_effects=True, vmem_limit_bytes=60 * 1024 * 1024
        ),
    )(
        row_block.reshape(1, rows),
        row_hits,
        row_slot.reshape(1, rows),
        track_kept.reshape(1, -1),
        row_derivs,
        row_resid,
        row_invsig,
        pattern,
        prior,
    )
    return out[0:1], out[1:2]


def solution(mesh):
    return jax.shard_map(
        functools.partial(on_device, owners=mesh.shape["blk"], shares=mesh.shape["trk"]),
        mesh=mesh,
        in_specs=(
            P(("blk", "trk"), None),
            P(None, ("blk", "trk")),
            P(("blk", "trk")),
            P(("blk", "trk")),
            P(None, ("blk", "trk")),
            P(("blk", "trk")),
            P(("blk", "trk")),
            P("blk", None),
            P("blk", None),
        ),
        out_specs=(P("blk", None), P("blk", None)),
        check_vma=False,
    )
```

```python
import functools

import jax
import jax.numpy as jnp
from jax import lax
from jax.experimental import pallas as pl
from jax.experimental.pallas import tpu as pltpu
from jax.sharding import PartitionSpec as P

MODS = 64
PAR = 6
NB = 5
SEG = 8
ITERS = 2


epsilon = 1e-06


def passed_along(block, axis, distance):
    devices = range(lax.axis_size(axis))
    route = [((i - distance) % len(devices), i) for i in devices]
    return lax.ppermute(block, axis, route)


def project(initial_norm, diag_terms, off_terms, basis_list):
    size_count = len(diag_terms)
    zero_value = diag_terms[0] * 0.0
    rows_list = []
    for row_index in range(size_count + 1):
        entries = []
        for column in range(size_count):
            if row_index == column:
                entries.append(diag_terms[column])
            elif row_index == column + 1:
                entries.append(off_terms[column])
            elif column == row_index + 1:
                entries.append(off_terms[row_index])
            else:
                entries.append(zero_value)
        rows_list.append(jnp.stack(entries))
    tridiagonal = jnp.stack(rows_list)
    gram_matrix = jnp.dot(tridiagonal.T, tridiagonal, precision=lax.Precision.HIGHEST)
    target = initial_norm * tridiagonal[0]
    factor = jnp.linalg.cholesky(gram_matrix)
    forward = []
    for row_index in range(size_count):
        partial_sum = target[row_index]
        for column in range(row_index):
            partial_sum = partial_sum - factor[row_index, column] * forward[column]
        forward.append(partial_sum / factor[row_index, row_index])
    backward = [zero_value] * size_count
    for row_index in reversed(range(size_count)):
        partial_sum = forward[row_index]
        for column in range(row_index + 1, size_count):
            partial_sum = partial_sum - factor[column, row_index] * backward[column]
        backward[row_index] = partial_sum / factor[row_index, row_index]
    solution = backward[0] * basis_list[0]
    row_index = 1
    solution = solution + backward[row_index] * basis_list[row_index]
    return solution


def contract(left_rows, right_rows):
    return lax.dot_general(
        left_rows, right_rows, (((0,), (0,)), ((), ())), preferred_element_type=jnp.float32
    )


def on_device_large(
    row_block, row_hits, row_slot, track_kept, row_derivs, row_resid, row_invsig, pattern, prior
):
    row_count = row_resid.shape[0]
    owners = lax.axis_size("blk")
    capacity = 2 * row_count // owners
    order_size = MODS * PAR
    kept_rows = jnp.repeat(track_kept, SEG).astype(jnp.float32)
    scaling = kept_rows * row_invsig.astype(jnp.float32)
    scaled = (scaling[None, :] * row_derivs.astype(jnp.float32)).astype(jnp.bfloat16)
    weighted = (scaling * row_resid.astype(jnp.float32)).astype(jnp.bfloat16)
    destination = row_block[:, 0]
    member = (destination[:, None] == jnp.arange(owners, dtype=jnp.int32)[None, :]).astype(
        jnp.bfloat16
    )
    row_ids = jnp.arange(row_count, dtype=jnp.int32)
    earlier = (row_ids[:, None] > row_ids[None, :]).astype(jnp.bfloat16)
    before = jnp.dot(earlier, member, preferred_element_type=jnp.float32)
    rank_within = jnp.sum(before * member.astype(jnp.float32), axis=1).astype(jnp.int32)
    slot_place = destination * capacity + rank_within
    labels = jnp.stack([row_hits[0], row_hits[1], row_slot]).astype(jnp.bfloat16)
    record = jnp.concatenate([scaled, weighted[None, :], labels], axis=0)
    outgoing = (
        jnp.zeros((record.shape[0], owners * capacity), jnp.bfloat16).at[:, slot_place].set(record)
    )
    incoming = lax.all_to_all(outgoing, "blk", split_axis=1, concat_axis=1, tiled=True)
    column_ids = jnp.arange(order_size, dtype=jnp.int32)
    column_module = column_ids // PAR
    column_param = column_ids % PAR

    def expand(values, module_ids):
        spread = jnp.zeros((values.shape[1], order_size), jnp.bfloat16)
        for component in range(PAR):
            spread = jnp.where(
                column_param[None, :] == component, values[component][:, None], spread
            )
        return jnp.where(
            module_ids[:, None] == column_module[None, :], spread, jnp.zeros_like(spread)
        )

    first_module = incoming[2 * PAR + 1].astype(jnp.int32)
    second_module = incoming[2 * PAR + 2].astype(jnp.int32)
    slot_in = incoming[2 * PAR + 3].astype(jnp.int32)
    resid_in = incoming[2 * PAR]
    first_rows = expand(incoming[0:PAR], first_module)
    second_rows = expand(incoming[PAR : 2 * PAR], second_module)
    own_block = contract(first_rows, first_rows)
    grad_own = jnp.dot(resid_in, first_rows, preferred_element_type=jnp.float32)
    cross_list, partner_list, grad_list = ([], [], [])
    for slot_id in range(NB):
        masked = jnp.where((slot_in == slot_id)[:, None], second_rows, jnp.zeros_like(second_rows))
        cross_list.append(contract(first_rows, masked))
        partner_list.append(contract(masked, masked))
        grad_list.append(jnp.dot(resid_in, masked, preferred_element_type=jnp.float32))
    cross_blocks = jnp.stack(cross_list)
    partner_blocks = jnp.stack(partner_list)
    grad_partner = jnp.stack(grad_list)
    position = lax.axis_index("blk")
    neighbours = pattern[0]
    offset = (neighbours - position) % owners
    offset = jnp.where(offset > owners // 2, offset - owners, offset)

    def deliver(own_term, partner_terms):
        local_sum = own_term + jnp.sum(
            jnp.where((offset == 0)[:, None], partner_terms, 0.0), axis=0, keepdims=True
        )
        for shift_by in (-2, -1, 1, 2):
            sending = jnp.sum(
                jnp.where((offset == shift_by)[:, None], partner_terms, 0.0), axis=0, keepdims=True
            )
            local_sum = local_sum + passed_along(sending, "blk", shift_by)
        return lax.psum(local_sum, "trk")

    gradient = deliver(grad_own[None, :], grad_partner)
    initial_norm = jnp.sqrt(lax.psum(jnp.sum(gradient * gradient), "blk") + epsilon)
    current = gradient / initial_norm
    previous = jnp.zeros_like(gradient)
    beta_term = jnp.zeros((), jnp.float32)
    diag_terms, off_terms, basis_list = ([], [], [])
    for iteration in range(ITERS):
        result = jnp.where((offset == 0)[:, None], current, 0.0)
        for fetch_shift_by in (-2, -1, 1, 2):
            arrived = passed_along(current, "blk", -fetch_shift_by)
            result = result + jnp.where((offset == fetch_shift_by)[:, None], arrived, 0.0)
        operate_own_term = jnp.dot(own_block, current[0], precision=lax.Precision.HIGHEST)
        operate_own_term = operate_own_term + jnp.einsum(
            "kij,kj->i", cross_blocks, result, precision=lax.Precision.HIGHEST
        )
        operate_partner_terms = jnp.einsum(
            "kij,i->kj", cross_blocks, current[0], precision=lax.Precision.HIGHEST
        )
        operate_partner_terms = operate_partner_terms + jnp.einsum(
            "kij,kj->ki", partner_blocks, result, precision=lax.Precision.HIGHEST
        )
        image_vec = prior * current + deliver(operate_own_term[None, :], operate_partner_terms)
        alpha_term = lax.psum(jnp.sum(current * image_vec), "blk")
        direction = image_vec - alpha_term * current - beta_term * previous
        beta_next = jnp.sqrt(lax.psum(jnp.sum(direction * direction), "blk") + epsilon)
        diag_terms.append(alpha_term)
        off_terms.append(beta_next)
        basis_list.append(current)
        previous, current, beta_term = (current, direction / beta_next, beta_next)
    solution = project(initial_norm, diag_terms, off_terms, basis_list)
    return (solution, gradient)


LANES = 128
WIDE = 8
PHASES = ITERS + 1
RECORD = 16
EXTRA = 3
MESH = pl.DeviceIdType.MESH


def three_parts(value):
    high = value.astype(jnp.bfloat16).astype(jnp.float32)
    rest = value - high
    middle = rest.astype(jnp.bfloat16).astype(jnp.float32)
    return jnp.concatenate([high, middle, rest - middle], axis=0).astype(jnp.bfloat16)


def two_parts(value, axis):
    high = value.astype(jnp.bfloat16)
    low = (value - high.astype(jnp.float32)).astype(jnp.bfloat16)
    return jnp.concatenate([high, low], axis=axis)


def total(value):
    return jnp.sum(jnp.sum(value, axis=0, keepdims=True), axis=1, keepdims=True)


def onehot(mask):
    return mask.astype(jnp.float32).astype(jnp.bfloat16)


def kernel(
    owners,
    shares,
    block_ref,
    hits_ref,
    slot_ref,
    kept_ref,
    derivs_ref,
    resid_ref,
    invsig_ref,
    pattern_ref,
    prior_ref,
    out_ref,
    block_in,
    hits_in,
    slot_in,
    kept_in,
    derivs_in,
    resid_in,
    invsig_in,
    pattern_in,
    prior_in,
    input_sem,
    record,
    extra,
    spread,
    labels,
    turned,
    products,
    mine,
    other,
    record_send,
    record_recv,
    extra_send,
    extra_recv,
    swap_send,
    swap_recv,
):
    blk, trk = lax.axis_index("blk"), lax.axis_index("trk")
    rows = block_ref.shape[1]
    tracks = kept_ref.shape[1]
    pairs = shares // 2
    pair, half = trk // 2, lax.rem(trk, 2)
    sibling = {"blk": blk, "trk": pair * 2 + 1 - half}
    order_size = MODS * PAR
    portion = order_size // shares

    me = blk * pairs + pair
    line = owners * pairs
    mirror = jnp.where(me < line // 2, 0, 1)
    place = jnp.where(mirror == 1, line - 1 - me, me)
    others = []
    for n in reversed(range(line - 1)):
        k = n + jnp.where(n >= place, 1, 0)
        others.append(jnp.where(mirror == 1, line - 1 - k, k))

    def peer(k):
        return {"blk": k // pairs, "trk": lax.rem(k, pairs) * 2 + half}

    peers = [peer(k) for k in others]
    barrier = pltpu.get_barrier_semaphore()
    for target in peers + [sibling]:
        pl.semaphore_signal(barrier, inc=1, device_id=target, device_id_type=MESH)

    outside = (
        kept_ref, invsig_ref, derivs_ref, resid_ref, block_ref, hits_ref, slot_ref, prior_ref, pattern_ref
    )
    inside = (
        kept_in, invsig_in, derivs_in, resid_in, block_in, hits_in, slot_in, prior_in, pattern_in
    )
    fetches = [
        pltpu.make_async_copy(source, target, input_sem.at[i])
        for i, (source, target) in enumerate(zip(outside, inside))
    ]
    for one in fetches:
        one.start()
    for one in fetches:
        one.wait()

    def copy(source, target, send, recv, device):
        return pltpu.make_async_remote_copy(
            src_ref=source, dst_ref=target, send_sem=send, recv_sem=recv, device_id=device, device_id_type=MESH
        )

    track_of = lax.broadcasted_iota(jnp.int32, (tracks, rows), 1) // SEG
    track_id = lax.broadcasted_iota(jnp.int32, (tracks, rows), 0)
    kept_rows = jnp.dot(
        onehot(jnp.broadcast_to(kept_in[...], (WIDE, tracks)) > 0),
        onehot(track_of == track_id),
        preferred_element_type=jnp.float32,
    )[0:1]
    scaling = kept_rows * invsig_in[...].reshape(1, rows).astype(jnp.float32)
    scaled = scaling * derivs_in[...].astype(jnp.float32)
    weighted = scaling * resid_in[...].reshape(1, rows).astype(jnp.float32)
    record[me] = jnp.concatenate(
        [scaled, weighted, hits_in[...].astype(jnp.float32), slot_in[...].astype(jnp.float32)], axis=0
    ).astype(jnp.bfloat16)
    block_row = block_in[...].astype(jnp.float32)
    for piece in range(rows // LANES):
        extra[me, piece : piece + 1] = block_row[:, piece * LANES : (piece + 1) * LANES]
    last = rows // LANES
    own = jnp.zeros((1, portion), jnp.float32)
    for t in range(shares):
        own = jnp.where(trk == t, prior_in[:, t * portion : (t + 1) * portion], own)
    extra[me, last : last + 1, 0:portion] = own
    extra[me, last : last + 1, portion : portion + NB] = pattern_in[...].astype(jnp.float32)

    pl.semaphore_wait(barrier, len(peers) + 1)
    sent = []
    for k, target in zip(others, peers):
        b, p = k // pairs, lax.rem(k, pairs)
        for data, send, recv in ((extra, extra_send, extra_recv), (record, record_send, record_recv)):
            sent.append(copy(data.at[me], data.at[me], send.at[b, p], recv.at[0], target))
    for one in sent:
        one.start()

    size = PAR * WIDE
    block_ids = lax.broadcasted_iota(jnp.int32, (WIDE, rows), 0).astype(jnp.float32)
    module_ids = lax.broadcasted_iota(jnp.int32, (MODS, 2 * rows), 0).astype(jnp.float32).astype(jnp.bfloat16)
    unit = jnp.ones((MODS, 2 * rows), jnp.bfloat16)
    rest_of = pl.ds(0, len(peers))
    for data, send, recv in ((extra, extra_send, extra_recv), (record, record_send, record_recv)):
        copy(data.at[rest_of], data.at[rest_of], send.at[0, 0], recv.at[0], sibling).wait_recv()
    side = [
        jnp.concatenate([extra[b * pairs + j, last : last + 1] for b in range(owners)], axis=0) for j in range(pairs)
    ]
    columns = [
        jnp.broadcast_to(side[0][:, portion + s : portion + s + 1], (WIDE, rows)) for s in range(NB)
    ]

    def prepare(b, p):
        values = record[b * pairs + p].astype(jnp.float32)
        first_block = jnp.concatenate([extra[b * pairs + p, i : i + 1] for i in range(last)], axis=1)
        first = block_ids == first_block
        slot = values[2 * PAR + 3 : 2 * PAR + 4]
        coupled = columns[0]
        for s in range(1, NB):
            coupled = jnp.where(slot == s, columns[s], coupled)
        second_block = jnp.sum(jnp.where(first, coupled, 0.0), axis=0, keepdims=True)
        second = block_ids == second_block
        terms = []
        for i in range(PAR):
            terms.append(
                jnp.concatenate(
                    [
                        jnp.where(first, values[i : i + 1], 0.0),
                        jnp.where(second, values[PAR + i : PAR + i + 1], 0.0),
                    ],
                    axis=1,
                )
            )
        terms = jnp.concatenate(terms, axis=0)
        spread[b, p] = terms
        labels_in = record[b * pairs + p, 2 * PAR : 2 * PAR + 3]
        weight = jnp.concatenate([labels_in[0:1], labels_in[0:1]], axis=1)
        hits = jnp.concatenate([labels_in[1:2], labels_in[2:3]], axis=1)
        match = module_ids == hits
        named = jnp.where(match, unit, jnp.zeros_like(unit))
        heavy = jnp.where(match, jnp.broadcast_to(weight, match.shape), jnp.zeros_like(unit))
        labels[b, p, 0:MODS] = named
        labels[b, p, MODS : 2 * MODS] = named
        turned[b, p] = jnp.transpose(jnp.concatenate([named, heavy], axis=0))
        k = b * pairs + p
        products[0:size, 2 * rows * k : 2 * rows * (k + 1)] = terms.astype(jnp.bfloat16)

    for k in range(owners * pairs):
        prepare(k // pairs, k % pairs)

    swaps = []

    def scattered(count):
        upright = turned[...].reshape(owners * pairs * 2 * rows, LANES)
        return jnp.dot(products[0:count], upright, preferred_element_type=jnp.float32)

    def exchange(phase, value, energy):
        mine[phase, 0:size] = value
        mine[phase, size:] = jnp.broadcast_to(energy, (WIDE, MODS))
        swap = copy(mine.at[phase], other.at[phase], swap_send.at[phase], swap_recv.at[phase], sibling)
        swap.start()
        swaps.append(swap)

    def received(phase):
        swaps[phase].wait_recv()
        both = mine[phase] + other[phase]
        return both[0:size], both[size : size + 1, 0:1]

    gradient = scattered(size)[:, MODS:]
    exchange(0, gradient, jnp.zeros((1, 1), jnp.float32))

    lane = lax.broadcasted_iota(jnp.int32, (LANES, order_size), 0)
    column = lax.broadcasted_iota(jnp.int32, (LANES, order_size), 1)
    prior = jnp.zeros((WIDE, order_size), jnp.float32)
    for j in range(pairs):
        module = lane // PAR + (2 * j + half) * (portion // PAR)
        place = onehot(
            (lane < portion) & (column == lax.rem(lane, PAR) * MODS + module)
        )
        laid = jnp.dot(three_parts(side[j]), place, preferred_element_type=jnp.float32)
        prior = prior + (laid[0:WIDE] + laid[WIDE : 2 * WIDE] + laid[2 * WIDE :])
    prior = jnp.concatenate([prior[:, i * MODS : (i + 1) * MODS] for i in range(PAR)], axis=0)

    def apply(phase, vector):
        parts = two_parts(vector, 1)
        energy = jnp.zeros((1, rows), jnp.float32)
        for k in range(owners * pairs):
            b, p = k // pairs, k % pairs
            terms = spread[b, p]
            read = jnp.dot(parts, labels[b, p], preferred_element_type=jnp.float32)
            along = jnp.sum(terms * read, axis=0, keepdims=True)
            along = along[:, 0:rows] + along[:, rows : 2 * rows]
            energy = energy + along * along
            products[:, 2 * rows * k : 2 * rows * (k + 1)] = two_parts(
                terms * jnp.concatenate([along, along], axis=1), 0
            )
        summed = scattered(2 * size)
        summed = summed[0:size, 0:MODS] + summed[size:, 0:MODS]
        damped = prior * vector
        exchange(phase, summed + damped, total(energy) + total(damped * vector))

    module_row = lax.broadcasted_iota(jnp.int32, (MODS, order_size), 0)
    module_of = lax.broadcasted_iota(jnp.int32, (MODS, order_size), 1) // PAR
    place = onehot(module_row == module_of)
    component = lax.broadcasted_iota(jnp.int32, (WIDE, order_size), 0)
    parameter = lax.broadcasted_iota(jnp.int32, (WIDE, order_size), 1)
    own_entry = component == lax.rem(parameter, PAR)
    own_block = lax.broadcasted_iota(jnp.int32, (WIDE, MODS), 0) == blk

    def in_order(vector):
        own = [
            jnp.sum(jnp.where(own_block, vector[i * WIDE : (i + 1) * WIDE], 0.0), axis=0, keepdims=True)
            for i in range(PAR)
        ]
        own = jnp.concatenate(own + [jnp.zeros((WIDE - PAR, MODS), jnp.float32)], axis=0)
        laid = jnp.dot(three_parts(own), place, preferred_element_type=jnp.float32)
        laid = laid[0:WIDE] + laid[WIDE : 2 * WIDE] + laid[2 * WIDE :]
        return jnp.sum(jnp.where(own_entry, laid, 0.0), axis=0, keepdims=True)

    for one in sent:
        one.wait_send()
    gradient, _ = received(0)
    apply(1, gradient)
    norm = total(gradient * gradient) + epsilon
    per_norm = 1.0 / norm
    laid_gradient = in_order(gradient)
    out_ref[1:2] = laid_gradient
    swaps[0].wait_send()
    image, energy = received(1)
    first = energy * per_norm
    direction = image - first * gradient
    apply(2, direction)
    scale = total(direction * direction) + epsilon * norm
    per_scale = 1.0 / scale
    below = scale * per_norm
    corner = first * first + below
    beyond = below * gradient
    laid_direction = in_order(direction)
    swaps[1].wait_send()
    image, energy = received(2)
    second = energy * per_scale
    rest = (image - beyond) - second * direction
    end = total(rest * rest) * per_scale + epsilon
    minor = first * second - below
    per_determinant = 1.0 / (minor * minor + end * corner)
    out_ref[0:1] = (
        ((second * minor + first * end) * per_determinant) * laid_gradient
        - (minor * per_determinant) * laid_direction
    )
    swaps[-1].wait_send()


def on_device(
    row_block,
    row_hits,
    row_slot,
    track_kept,
    row_derivs,
    row_resid,
    row_invsig,
    pattern,
    prior,
    owners,
    shares,
):
    args = (
        row_block, row_hits, row_slot, track_kept, row_derivs, row_resid, row_invsig, pattern, prior
    )
    if owners != WIDE or 2 * MODS != LANES or shares % 2 or MODS % shares:
        return on_device_large(*args)
    rows = row_resid.shape[0]
    dma = pltpu.SemaphoreType.DMA
    pairs = shares // 2
    out = pl.pallas_call(
        functools.partial(kernel, owners, shares),
        out_shape=pltpu.VMEM((2, MODS * PAR), jnp.float32),
        in_specs=[pl.BlockSpec(memory_space=pltpu.HBM)] * 9,
        out_specs=pl.BlockSpec(memory_space=pltpu.VMEM),
        scratch_shapes=[
            pltpu.VMEM((1, rows), jnp.int32),
            pltpu.VMEM((2, rows), jnp.int32),
            pltpu.VMEM((1, rows), jnp.int32),
            pltpu.VMEM((1, track_kept.shape[0]), jnp.int32),
            pltpu.VMEM((2 * PAR, rows), jnp.bfloat16),
            pltpu.VMEM((rows,), jnp.bfloat16),
            pltpu.VMEM((rows,), jnp.bfloat16),
            pltpu.VMEM((1, NB), jnp.int32),
            pltpu.VMEM((1, MODS * PAR), jnp.float32),
            dma((9,)),
            pltpu.VMEM((owners * pairs, RECORD, rows), jnp.bfloat16),
            pltpu.VMEM((owners * pairs, EXTRA, LANES), jnp.float32),
            pltpu.VMEM((owners, pairs, PAR * WIDE, 2 * rows), jnp.float32),
            pltpu.VMEM((owners, pairs, 2 * MODS, 2 * rows), jnp.bfloat16),
            pltpu.VMEM((owners, pairs, 2 * rows, LANES), jnp.bfloat16),
            pltpu.VMEM((2 * PAR * WIDE, owners * pairs * 2 * rows), jnp.bfloat16),
            pltpu.VMEM((PHASES, PAR * WIDE + WIDE, MODS), jnp.float32),
            pltpu.VMEM((PHASES, PAR * WIDE + WIDE, MODS), jnp.float32),
            dma((owners, pairs)),
            dma((1,)),
            dma((owners, pairs)),
            dma((1,)),
            dma((PHASES,)),
            dma((PHASES,)),
        ],
        compiler_params=pltpu.CompilerParams(
            collective_id=0, has_side_effects=True, vmem_limit_bytes=60 * 1024 * 1024
        ),
    )(
        row_block.reshape(1, rows),
        row_hits,
        row_slot.reshape(1, rows),
        track_kept.reshape(1, -1),
        row_derivs,
        row_resid,
        row_invsig,
        pattern,
        prior,
    )
    return out[0:1], out[1:2]


def solution(mesh):
    return jax.shard_map(
        functools.partial(on_device, owners=mesh.shape["blk"], shares=mesh.shape["trk"]),
        mesh=mesh,
        in_specs=(
            P(("blk", "trk"), None),
            P(None, ("blk", "trk")),
            P(("blk", "trk")),
            P(("blk", "trk")),
            P(None, ("blk", "trk")),
            P(("blk", "trk")),
            P(("blk", "trk")),
            P("blk", None),
            P("blk", None),
        ),
        out_specs=(P("blk", None), P("blk", None)),
        check_vma=False,
    )
```

```python
import functools

import jax
import jax.numpy as jnp
from jax import lax
from jax.experimental import pallas as pl
from jax.experimental.pallas import tpu as pltpu
from jax.sharding import PartitionSpec as P

MODS = 64
PAR = 6
NB = 5
SEG = 8
ITERS = 2


epsilon = 1e-06


def passed_along(block, axis, distance):
    devices = range(lax.axis_size(axis))
    route = [((i - distance) % len(devices), i) for i in devices]
    return lax.ppermute(block, axis, route)


def project(initial_norm, diag_terms, off_terms, basis_list):
    size_count = len(diag_terms)
    zero_value = diag_terms[0] * 0.0
    rows_list = []
    for row_index in range(size_count + 1):
        entries = []
        for column in range(size_count):
            if row_index == column:
                entries.append(diag_terms[column])
            elif row_index == column + 1:
                entries.append(off_terms[column])
            elif column == row_index + 1:
                entries.append(off_terms[row_index])
            else:
                entries.append(zero_value)
        rows_list.append(jnp.stack(entries))
    tridiagonal = jnp.stack(rows_list)
    gram_matrix = jnp.dot(tridiagonal.T, tridiagonal, precision=lax.Precision.HIGHEST)
    target = initial_norm * tridiagonal[0]
    factor = jnp.linalg.cholesky(gram_matrix)
    forward = []
    for row_index in range(size_count):
        partial_sum = target[row_index]
        for column in range(row_index):
            partial_sum = partial_sum - factor[row_index, column] * forward[column]
        forward.append(partial_sum / factor[row_index, row_index])
    backward = [zero_value] * size_count
    for row_index in reversed(range(size_count)):
        partial_sum = forward[row_index]
        for column in range(row_index + 1, size_count):
            partial_sum = partial_sum - factor[column, row_index] * backward[column]
        backward[row_index] = partial_sum / factor[row_index, row_index]
    solution = backward[0] * basis_list[0]
    row_index = 1
    solution = solution + backward[row_index] * basis_list[row_index]
    return solution


def contract(left_rows, right_rows):
    return lax.dot_general(
        left_rows, right_rows, (((0,), (0,)), ((), ())), preferred_element_type=jnp.float32
    )


def on_device_large(
    row_block, row_hits, row_slot, track_kept, row_derivs, row_resid, row_invsig, pattern, prior
):
    row_count = row_resid.shape[0]
    owners = lax.axis_size("blk")
    capacity = 2 * row_count // owners
    order_size = MODS * PAR
    kept_rows = jnp.repeat(track_kept, SEG).astype(jnp.float32)
    scaling = kept_rows * row_invsig.astype(jnp.float32)
    scaled = (scaling[None, :] * row_derivs.astype(jnp.float32)).astype(jnp.bfloat16)
    weighted = (scaling * row_resid.astype(jnp.float32)).astype(jnp.bfloat16)
    destination = row_block[:, 0]
    member = (destination[:, None] == jnp.arange(owners, dtype=jnp.int32)[None, :]).astype(
        jnp.bfloat16
    )
    row_ids = jnp.arange(row_count, dtype=jnp.int32)
    earlier = (row_ids[:, None] > row_ids[None, :]).astype(jnp.bfloat16)
    before = jnp.dot(earlier, member, preferred_element_type=jnp.float32)
    rank_within = jnp.sum(before * member.astype(jnp.float32), axis=1).astype(jnp.int32)
    slot_place = destination * capacity + rank_within
    labels = jnp.stack([row_hits[0], row_hits[1], row_slot]).astype(jnp.bfloat16)
    record = jnp.concatenate([scaled, weighted[None, :], labels], axis=0)
    outgoing = (
        jnp.zeros((record.shape[0], owners * capacity), jnp.bfloat16).at[:, slot_place].set(record)
    )
    incoming = lax.all_to_all(outgoing, "blk", split_axis=1, concat_axis=1, tiled=True)
    column_ids = jnp.arange(order_size, dtype=jnp.int32)
    column_module = column_ids // PAR
    column_param = column_ids % PAR

    def expand(values, module_ids):
        spread = jnp.zeros((values.shape[1], order_size), jnp.bfloat16)
        for component in range(PAR):
            spread = jnp.where(
                column_param[None, :] == component, values[component][:, None], spread
            )
        return jnp.where(
            module_ids[:, None] == column_module[None, :], spread, jnp.zeros_like(spread)
        )

    first_module = incoming[2 * PAR + 1].astype(jnp.int32)
    second_module = incoming[2 * PAR + 2].astype(jnp.int32)
    slot_in = incoming[2 * PAR + 3].astype(jnp.int32)
    resid_in = incoming[2 * PAR]
    first_rows = expand(incoming[0:PAR], first_module)
    second_rows = expand(incoming[PAR : 2 * PAR], second_module)
    own_block = contract(first_rows, first_rows)
    grad_own = jnp.dot(resid_in, first_rows, preferred_element_type=jnp.float32)
    cross_list, partner_list, grad_list = ([], [], [])
    for slot_id in range(NB):
        masked = jnp.where((slot_in == slot_id)[:, None], second_rows, jnp.zeros_like(second_rows))
        cross_list.append(contract(first_rows, masked))
        partner_list.append(contract(masked, masked))
        grad_list.append(jnp.dot(resid_in, masked, preferred_element_type=jnp.float32))
    cross_blocks = jnp.stack(cross_list)
    partner_blocks = jnp.stack(partner_list)
    grad_partner = jnp.stack(grad_list)
    position = lax.axis_index("blk")
    neighbours = pattern[0]
    offset = (neighbours - position) % owners
    offset = jnp.where(offset > owners // 2, offset - owners, offset)

    def deliver(own_term, partner_terms):
        local_sum = own_term + jnp.sum(
            jnp.where((offset == 0)[:, None], partner_terms, 0.0), axis=0, keepdims=True
        )
        for shift_by in (-2, -1, 1, 2):
            sending = jnp.sum(
                jnp.where((offset == shift_by)[:, None], partner_terms, 0.0), axis=0, keepdims=True
            )
            local_sum = local_sum + passed_along(sending, "blk", shift_by)
        return lax.psum(local_sum, "trk")

    gradient = deliver(grad_own[None, :], grad_partner)
    initial_norm = jnp.sqrt(lax.psum(jnp.sum(gradient * gradient), "blk") + epsilon)
    current = gradient / initial_norm
    previous = jnp.zeros_like(gradient)
    beta_term = jnp.zeros((), jnp.float32)
    diag_terms, off_terms, basis_list = ([], [], [])
    for iteration in range(ITERS):
        result = jnp.where((offset == 0)[:, None], current, 0.0)
        for fetch_shift_by in (-2, -1, 1, 2):
            arrived = passed_along(current, "blk", -fetch_shift_by)
            result = result + jnp.where((offset == fetch_shift_by)[:, None], arrived, 0.0)
        operate_own_term = jnp.dot(own_block, current[0], precision=lax.Precision.HIGHEST)
        operate_own_term = operate_own_term + jnp.einsum(
            "kij,kj->i", cross_blocks, result, precision=lax.Precision.HIGHEST
        )
        operate_partner_terms = jnp.einsum(
            "kij,i->kj", cross_blocks, current[0], precision=lax.Precision.HIGHEST
        )
        operate_partner_terms = operate_partner_terms + jnp.einsum(
            "kij,kj->ki", partner_blocks, result, precision=lax.Precision.HIGHEST
        )
        image_vec = prior * current + deliver(operate_own_term[None, :], operate_partner_terms)
        alpha_term = lax.psum(jnp.sum(current * image_vec), "blk")
        direction = image_vec - alpha_term * current - beta_term * previous
        beta_next = jnp.sqrt(lax.psum(jnp.sum(direction * direction), "blk") + epsilon)
        diag_terms.append(alpha_term)
        off_terms.append(beta_next)
        basis_list.append(current)
        previous, current, beta_term = (current, direction / beta_next, beta_next)
    solution = project(initial_norm, diag_terms, off_terms, basis_list)
    return (solution, gradient)


LANES = 128
WIDE = 8
PHASES = ITERS + 1
RECORD = 16
EXTRA = 3
MESH = pl.DeviceIdType.MESH


def three_parts(value):
    high = value.astype(jnp.bfloat16).astype(jnp.float32)
    rest = value - high
    middle = rest.astype(jnp.bfloat16).astype(jnp.float32)
    return jnp.concatenate([high, middle, rest - middle], axis=0).astype(jnp.bfloat16)


def two_parts(value, axis):
    high = value.astype(jnp.bfloat16)
    low = (value - high.astype(jnp.float32)).astype(jnp.bfloat16)
    return jnp.concatenate([high, low], axis=axis)


def total(value):
    return jnp.sum(jnp.sum(value, axis=0, keepdims=True), axis=1, keepdims=True)


def onehot(mask):
    return mask.astype(jnp.float32).astype(jnp.bfloat16)


def kernel(
    owners,
    shares,
    block_ref,
    hits_ref,
    slot_ref,
    kept_ref,
    derivs_ref,
    resid_ref,
    invsig_ref,
    pattern_ref,
    prior_ref,
    out_ref,
    block_in,
    hits_in,
    slot_in,
    kept_in,
    derivs_in,
    resid_in,
    invsig_in,
    pattern_in,
    prior_in,
    input_sem,
    record,
    extra,
    spread,
    labels,
    turned,
    products,
    mine,
    other,
    record_send,
    record_recv,
    extra_send,
    extra_recv,
    swap_send,
    swap_recv,
):
    blk, trk = lax.axis_index("blk"), lax.axis_index("trk")
    rows = block_ref.shape[1]
    tracks = kept_ref.shape[1]
    pairs = shares // 2
    pair, half = trk // 2, lax.rem(trk, 2)
    sibling = {"blk": blk, "trk": pair * 2 + 1 - half}
    order_size = MODS * PAR
    portion = order_size // shares

    me = blk * pairs + pair
    line = owners * pairs
    mirror = jnp.where(me < line // 2, 0, 1)
    place = jnp.where(mirror == 1, line - 1 - me, me)
    others = []
    for n in reversed(range(line - 1)):
        k = n + jnp.where(n >= place, 1, 0)
        others.append(jnp.where(mirror == 1, line - 1 - k, k))

    def peer(k):
        return {"blk": k // pairs, "trk": lax.rem(k, pairs) * 2 + half}

    peers = [peer(k) for k in others]
    barrier = pltpu.get_barrier_semaphore()
    for target in peers + [sibling]:
        pl.semaphore_signal(barrier, inc=1, device_id=target, device_id_type=MESH)

    outside = (
        kept_ref, invsig_ref, derivs_ref, resid_ref, block_ref, hits_ref, slot_ref, prior_ref, pattern_ref
    )
    inside = (
        kept_in, invsig_in, derivs_in, resid_in, block_in, hits_in, slot_in, prior_in, pattern_in
    )
    fetches = [
        pltpu.make_async_copy(source, target, input_sem.at[i])
        for i, (source, target) in enumerate(zip(outside, inside))
    ]
    for one in fetches:
        one.start()
    for one in fetches:
        one.wait()

    def copy(source, target, send, recv, device):
        return pltpu.make_async_remote_copy(
            src_ref=source, dst_ref=target, send_sem=send, recv_sem=recv, device_id=device, device_id_type=MESH
        )

    track_of = lax.broadcasted_iota(jnp.int32, (tracks, rows), 1) // SEG
    track_id = lax.broadcasted_iota(jnp.int32, (tracks, rows), 0)
    kept_rows = jnp.dot(
        onehot(jnp.broadcast_to(kept_in[...], (WIDE, tracks)) > 0),
        onehot(track_of == track_id),
        preferred_element_type=jnp.float32,
    )[0:1]
    scaling = kept_rows * invsig_in[...].reshape(1, rows).astype(jnp.float32)
    scaled = scaling * derivs_in[...].astype(jnp.float32)
    weighted = scaling * resid_in[...].reshape(1, rows).astype(jnp.float32)
    record[me] = jnp.concatenate(
        [scaled, weighted, hits_in[...].astype(jnp.float32), slot_in[...].astype(jnp.float32)], axis=0
    ).astype(jnp.bfloat16)
    block_row = block_in[...].astype(jnp.float32)
    for piece in range(rows // LANES):
        extra[me, piece : piece + 1] = block_row[:, piece * LANES : (piece + 1) * LANES]
    last = rows // LANES
    own = jnp.zeros((1, portion), jnp.float32)
    for t in range(shares):
        own = jnp.where(trk == t, prior_in[:, t * portion : (t + 1) * portion], own)
    extra[me, last : last + 1, 0:portion] = own
    extra[me, last : last + 1, portion : portion + NB] = pattern_in[...].astype(jnp.float32)

    pl.semaphore_wait(barrier, len(peers) + 1)
    sent = []
    for k, target in zip(others, peers):
        b, p = k // pairs, lax.rem(k, pairs)
        for data, send, recv in ((extra, extra_send, extra_recv), (record, record_send, record_recv)):
            sent.append(copy(data.at[me], data.at[me], send.at[b, p], recv.at[0], target))
    for one in sent:
        one.start()

    size = PAR * WIDE
    block_ids = lax.broadcasted_iota(jnp.int32, (WIDE, rows), 0).astype(jnp.float32)
    module_ids = lax.broadcasted_iota(jnp.int32, (MODS, 2 * rows), 0).astype(jnp.float32).astype(jnp.bfloat16)
    unit = jnp.ones((MODS, 2 * rows), jnp.bfloat16)
    rest_of = pl.ds(0, len(peers))
    for data, send, recv in ((extra, extra_send, extra_recv), (record, record_send, record_recv)):
        copy(data.at[rest_of], data.at[rest_of], send.at[0, 0], recv.at[0], sibling).wait_recv()
    side = [
        jnp.concatenate([extra[b * pairs + j, last : last + 1] for b in range(owners)], axis=0) for j in range(pairs)
    ]
    columns = [
        jnp.broadcast_to(side[0][:, portion + s : portion + s + 1], (WIDE, rows)) for s in range(NB)
    ]

    def prepare(b, p):
        values = record[b * pairs + p].astype(jnp.float32)
        first_block = jnp.concatenate([extra[b * pairs + p, i : i + 1] for i in range(last)], axis=1)
        first = block_ids == first_block
        slot = values[2 * PAR + 3 : 2 * PAR + 4]
        coupled = columns[0]
        for s in range(1, NB):
            coupled = jnp.where(slot == s, columns[s], coupled)
        second_block = jnp.sum(jnp.where(first, coupled, 0.0), axis=0, keepdims=True)
        second = block_ids == second_block
        terms = []
        for i in range(PAR):
            terms.append(
                jnp.concatenate(
                    [
                        jnp.where(first, values[i : i + 1], 0.0),
                        jnp.where(second, values[PAR + i : PAR + i + 1], 0.0),
                    ],
                    axis=1,
                )
            )
        terms = jnp.concatenate(terms, axis=0)
        spread[b, p] = terms
        labels_in = record[b * pairs + p, 2 * PAR : 2 * PAR + 3]
        weight = jnp.concatenate([labels_in[0:1], labels_in[0:1]], axis=1)
        hits = jnp.concatenate([labels_in[1:2], labels_in[2:3]], axis=1)
        match = module_ids == hits
        named = jnp.where(match, unit, jnp.zeros_like(unit))
        heavy = jnp.where(match, jnp.broadcast_to(weight, match.shape), jnp.zeros_like(unit))
        labels[b, p, 0:MODS] = named
        labels[b, p, MODS : 2 * MODS] = named
        turned[b, p] = jnp.transpose(jnp.concatenate([named, heavy], axis=0))
        k = b * pairs + p
        products[0:size, 2 * rows * k : 2 * rows * (k + 1)] = terms.astype(jnp.bfloat16)

    for k in range(owners * pairs):
        prepare(k // pairs, k % pairs)

    swaps = []

    def scattered(count):
        upright = turned[...].reshape(owners * pairs * 2 * rows, LANES)
        return jnp.dot(products[0:count], upright, preferred_element_type=jnp.float32)

    def exchange(phase, value, energy):
        mine[phase, 0:size] = value
        mine[phase, size:] = jnp.broadcast_to(energy, (WIDE, MODS))
        swap = copy(mine.at[phase], other.at[phase], swap_send.at[phase], swap_recv.at[phase], sibling)
        swap.start()
        swaps.append(swap)

    def received(phase):
        swaps[phase].wait_recv()
        both = mine[phase] + other[phase]
        return both[0:size], both[size : size + 1, 0:1]

    gradient = scattered(size)[:, MODS:]
    exchange(0, gradient, jnp.zeros((1, 1), jnp.float32))

    lane = lax.broadcasted_iota(jnp.int32, (LANES, order_size), 0)
    column = lax.broadcasted_iota(jnp.int32, (LANES, order_size), 1)
    prior = jnp.zeros((WIDE, order_size), jnp.float32)
    for j in range(pairs):
        module = lane // PAR + (2 * j + half) * (portion // PAR)
        place = onehot(
            (lane < portion) & (column == lax.rem(lane, PAR) * MODS + module)
        )
        laid = jnp.dot(three_parts(side[j]), place, preferred_element_type=jnp.float32)
        prior = prior + (laid[0:WIDE] + laid[WIDE : 2 * WIDE] + laid[2 * WIDE :])
    prior = jnp.concatenate([prior[:, i * MODS : (i + 1) * MODS] for i in range(PAR)], axis=0)

    def apply(phase, vector):
        parts = two_parts(vector, 1)
        energy = jnp.zeros((1, rows), jnp.float32)
        summed = jnp.zeros((2 * size, LANES), jnp.float32)
        chunk = owners * pairs // 2
        for k in range(owners * pairs):
            b, p = k // pairs, k % pairs
            terms = spread[b, p]
            read = jnp.dot(parts, labels[b, p], preferred_element_type=jnp.float32)
            along = jnp.sum(terms * read, axis=0, keepdims=True)
            along = along[:, 0:rows] + along[:, rows : 2 * rows]
            energy = energy + along * along
            products[:, 2 * rows * k : 2 * rows * (k + 1)] = two_parts(
                terms * jnp.concatenate([along, along], axis=1), 0
            )
            if k % chunk == chunk - 1:
                begin = k + 1 - chunk
                upright = turned[begin // pairs : (k + 1) // pairs].reshape(chunk * 2 * rows, LANES)
                summed = summed + jnp.dot(
                    products[:, 2 * rows * begin : 2 * rows * (k + 1)], upright, preferred_element_type=jnp.float32
                )
        summed = summed[0:size, 0:MODS] + summed[size:, 0:MODS]
        damped = prior * vector
        exchange(phase, summed + damped, total(energy) + total(damped * vector))

    module_row = lax.broadcasted_iota(jnp.int32, (MODS, order_size), 0)
    module_of = lax.broadcasted_iota(jnp.int32, (MODS, order_size), 1) // PAR
    place = onehot(module_row == module_of)
    component = lax.broadcasted_iota(jnp.int32, (WIDE, order_size), 0)
    parameter = lax.broadcasted_iota(jnp.int32, (WIDE, order_size), 1)
    own_entry = component == lax.rem(parameter, PAR)
    own_block = lax.broadcasted_iota(jnp.int32, (WIDE, MODS), 0) == blk

    def in_order(vector):
        own = [
            jnp.sum(jnp.where(own_block, vector[i * WIDE : (i + 1) * WIDE], 0.0), axis=0, keepdims=True)
            for i in range(PAR)
        ]
        own = jnp.concatenate(own + [jnp.zeros((WIDE - PAR, MODS), jnp.float32)], axis=0)
        laid = jnp.dot(three_parts(own), place, preferred_element_type=jnp.float32)
        laid = laid[0:WIDE] + laid[WIDE : 2 * WIDE] + laid[2 * WIDE :]
        return jnp.sum(jnp.where(own_entry, laid, 0.0), axis=0, keepdims=True)

    for one in sent:
        one.wait_send()
    gradient, _ = received(0)
    apply(1, gradient)
    norm = total(gradient * gradient) + epsilon
    per_norm = 1.0 / norm
    laid_gradient = in_order(gradient)
    out_ref[1:2] = laid_gradient
    swaps[0].wait_send()
    image, energy = received(1)
    first = energy * per_norm
    direction = image - first * gradient
    apply(2, direction)
    scale = total(direction * direction) + epsilon * norm
    per_scale = 1.0 / scale
    below = scale * per_norm
    corner = first * first + below
    beyond = below * gradient
    laid_direction = in_order(direction)
    swaps[1].wait_send()
    image, energy = received(2)
    second = energy * per_scale
    rest = (image - beyond) - second * direction
    end = total(rest * rest) * per_scale + epsilon
    minor = first * second - below
    per_determinant = 1.0 / (minor * minor + end * corner)
    out_ref[0:1] = (
        ((second * minor + first * end) * per_determinant) * laid_gradient
        - (minor * per_determinant) * laid_direction
    )
    swaps[-1].wait_send()


def on_device(
    row_block,
    row_hits,
    row_slot,
    track_kept,
    row_derivs,
    row_resid,
    row_invsig,
    pattern,
    prior,
    owners,
    shares,
):
    args = (
        row_block, row_hits, row_slot, track_kept, row_derivs, row_resid, row_invsig, pattern, prior
    )
    if owners != WIDE or 2 * MODS != LANES or shares % 2 or MODS % shares:
        return on_device_large(*args)
    rows = row_resid.shape[0]
    dma = pltpu.SemaphoreType.DMA
    pairs = shares // 2
    out = pl.pallas_call(
        functools.partial(kernel, owners, shares),
        out_shape=pltpu.VMEM((2, MODS * PAR), jnp.float32),
        in_specs=[pl.BlockSpec(memory_space=pltpu.HBM)] * 9,
        out_specs=pl.BlockSpec(memory_space=pltpu.VMEM),
        scratch_shapes=[
            pltpu.VMEM((1, rows), jnp.int32),
            pltpu.VMEM((2, rows), jnp.int32),
            pltpu.VMEM((1, rows), jnp.int32),
            pltpu.VMEM((1, track_kept.shape[0]), jnp.int32),
            pltpu.VMEM((2 * PAR, rows), jnp.bfloat16),
            pltpu.VMEM((rows,), jnp.bfloat16),
            pltpu.VMEM((rows,), jnp.bfloat16),
            pltpu.VMEM((1, NB), jnp.int32),
            pltpu.VMEM((1, MODS * PAR), jnp.float32),
            dma((9,)),
            pltpu.VMEM((owners * pairs, RECORD, rows), jnp.bfloat16),
            pltpu.VMEM((owners * pairs, EXTRA, LANES), jnp.float32),
            pltpu.VMEM((owners, pairs, PAR * WIDE, 2 * rows), jnp.float32),
            pltpu.VMEM((owners, pairs, 2 * MODS, 2 * rows), jnp.bfloat16),
            pltpu.VMEM((owners, pairs, 2 * rows, LANES), jnp.bfloat16),
            pltpu.VMEM((2 * PAR * WIDE, owners * pairs * 2 * rows), jnp.bfloat16),
            pltpu.VMEM((PHASES, PAR * WIDE + WIDE, MODS), jnp.float32),
            pltpu.VMEM((PHASES, PAR * WIDE + WIDE, MODS), jnp.float32),
            dma((owners, pairs)),
            dma((1,)),
            dma((owners, pairs)),
            dma((1,)),
            dma((PHASES,)),
            dma((PHASES,)),
        ],
        compiler_params=pltpu.CompilerParams(
            collective_id=0, has_side_effects=True, vmem_limit_bytes=60 * 1024 * 1024
        ),
    )(
        row_block.reshape(1, rows),
        row_hits,
        row_slot.reshape(1, rows),
        track_kept.reshape(1, -1),
        row_derivs,
        row_resid,
        row_invsig,
        pattern,
        prior,
    )
    return out[0:1], out[1:2]


def solution(mesh):
    return jax.shard_map(
        functools.partial(on_device, owners=mesh.shape["blk"], shares=mesh.shape["trk"]),
        mesh=mesh,
        in_specs=(
            P(("blk", "trk"), None),
            P(None, ("blk", "trk")),
            P(("blk", "trk")),
            P(("blk", "trk")),
            P(None, ("blk", "trk")),
            P(("blk", "trk")),
            P(("blk", "trk")),
            P("blk", None),
            P("blk", None),
        ),
        out_specs=(P("blk", None), P("blk", None)),
        check_vma=False,
    )
```
